256 devices in a mesh: gx: 64 (over z, x, y_hi), gy: 4 (over y_lo, core).
Axes of the slice: x: 4, y: 4 (y_hi: 2, y_lo: 2; y = y_hi * 2 + y_lo), z: 8, core: 2. Of those that a mesh axis runs over, the one named last changes fastest.
Arguments:
- positions: float32 [3, 32768], P(None, ('gx', 'gy')), may hold values from 0 to 4
- velocities: float32 [3, 32768], P(None, ('gx', 'gy')), may hold values from -3 to 3
- species: int32 [32768], P(('gx', 'gy')), may hold values from 0 to 3
- counts: int32 [32768], P(('gx', 'gy')), may hold values from 3 to 12
- neighbours: int32 [12, 32768], P(None, ('gx', 'gy')), may hold values from 0 to 639
- send_lists: int32 [4, 16384], P(None, ('gx', 'gy')), may hold values from 0 to 127
- inv_mass: float32 [4], replicated, may hold values from 0.5 to 2
- w_rad_one: float32 [4, 8, 256], replicated, may hold values from -2 to 2
- emb_nbr: float32 [4, 4, 256], replicated, may hold values from -4 to 4
- emb_self: float32 [4, 4, 256], replicated, may hold values from -4 to 4
- w_one: float32 [4, 256, 256], replicated, may hold values from -0.375 to 0.375
- w_src: float32 [4, 256, 256], replicated, may hold values from -0.375 to 0.375
- w_dst: float32 [4, 256, 256], replicated, may hold values from -0.375 to 0.375
- w_rad_two: float32 [4, 8, 256], replicated, may hold values from -2 to 2
- w_edge: float32 [4, 256, 256], replicated, may hold values from -0.375 to 0.375
- w_out: float32 [4, 256], replicated, may hold values from -0.375 to 0.375
Outputs:
- new_positions: float32 [3, 32768], P(None, ('gx', 'gy'))
- new_velocities: float32 [3, 32768], P(None, ('gx', 'gy'))
The draws below stay inside these ranges and needn't reach their ends.
Inputs may be any that keep to these rules, and one draw needn't show every extreme that they name: `neighbours`: entries index a sub-box's extended list: its owned atoms first, then the 8 ghost blocks in the stated order. `counts`: slots at or beyond an atom's count are padding. `send_lists`: an atom may stand in several lists or several times in one.
All inputs are finite; a program needn't handle non-finite values.
Results may differ from the reference program's by a relative error of at most 0.0003.
Values sent between devices are 32-bit elements; how exact they have to be, the bound alone decides.
No kernel may reach another device: no remote copies, remote signals or barrier semaphores. Data moves between devices by JAX's collectives and lax.ppermute only.
A program may use at most 128 MiB of HBM per device.

```python
import math
import jax
import jax.numpy as jnp
from jax import lax

LATENT = 256
RADIAL = 8
SPECIES = 4
MEMBERS = 4
NEIGHBOURS = 12
ATOMS_DEV = 128
GHOSTS = 64
ATOMS = 32768
SENDS = 16384
SLOTS = 640
N_GX = 64
N_GY = 4


def set_ends(drawn, own_key, least, largest):
    longest = drawn.shape.index(max(drawn.shape))
    spots = []
    for shift in (0, 1):
        where = [jax.random.randint(jax.random.fold_in(own_key, axis), (), 0, length) for axis, length in enumerate(drawn.shape)]
        where[longest] = (where[longest] + shift) % drawn.shape[longest]
        spots.append(tuple(where))
    return drawn.at[spots[0]].set(least).at[spots[1]].set(largest)


def block_scale(key, extent, shards, smallest, high):
    loudness, own = 1.0, jax.random.fold_in(key, 6)
    for position, shards_of in shards:
        steps = jnp.exp(jax.random.uniform(jax.random.fold_in(own, position), (shards_of,), jnp.float32, smallest / len(shards), high / len(shards)))
        loudness = loudness * jnp.repeat(steps, extent[position] // shards_of).reshape([-1 if axis == position else 1 for axis in range(len(extent))])
    return loudness


def gaussian(rng, extent, spread, bound, pieces=(), kind=jnp.bfloat16):
    values = spread * jax.random.normal(rng, extent, jnp.float32)
    if pieces:
        values = values * block_scale(rng, extent, pieces, -0.22, 0.18)
    return jnp.clip(values, -bound, bound).astype(kind)


def setup_inputs(seed: int = 0) -> dict:
    keys = jax.random.split(jax.random.key(seed), 17)
    positions = jnp.clip(4.0 * jax.random.uniform(keys[0], (3, ATOMS), jnp.float32) ** block_scale(keys[0], (3, ATOMS), ((1, 256),), -0.2, 0.2), 0.0, 4.0)
    velocities = gaussian(keys[1], (3, ATOMS), 0.5, 3.0, ((1, 256),), jnp.float32)
    species = set_ends(jax.random.randint(keys[2], (ATOMS,), 0, SPECIES), jax.random.fold_in(keys[2], 1), 0, SPECIES - 1).astype(jnp.int32)
    counts = set_ends(jax.random.randint(keys[3], (ATOMS,), NEIGHBOURS // 4, NEIGHBOURS + 1), jax.random.fold_in(keys[3], 1), NEIGHBOURS // 4, NEIGHBOURS).astype(jnp.int32)
    neighbours = set_ends(jax.random.randint(keys[4], (NEIGHBOURS, ATOMS), 0, SLOTS), jax.random.fold_in(keys[4], 1), 0, SLOTS - 1).astype(jnp.int32)
    send_lists = set_ends(jax.random.randint(keys[5], (4, SENDS), 0, ATOMS_DEV), jax.random.fold_in(keys[5], 1), 0, ATOMS_DEV - 1).astype(jnp.int32)
    inv_mass = jnp.clip(jnp.exp(jax.random.uniform(keys[6], (SPECIES,), jnp.float32, math.log(0.5), math.log(2.0))), 0.5, 2.0)
    w_rad_one = gaussian(keys[7], (MEMBERS, RADIAL, LATENT), RADIAL ** -0.5, 2.0, (), jnp.float32)
    emb_nbr = gaussian(keys[8], (MEMBERS, SPECIES, LATENT), 1.0, 4.0, (), jnp.float32)
    emb_self = gaussian(keys[9], (MEMBERS, SPECIES, LATENT), 1.0, 4.0, (), jnp.float32)
    w_one = gaussian(keys[10], (MEMBERS, LATENT, LATENT), LATENT ** -0.5, 0.375, (), jnp.float32)
    w_src = gaussian(keys[11], (MEMBERS, LATENT, LATENT), LATENT ** -0.5, 0.375, (), jnp.float32)
    w_dst = gaussian(keys[12], (MEMBERS, LATENT, LATENT), LATENT ** -0.5, 0.375, (), jnp.float32)
    w_rad_two = gaussian(keys[13], (MEMBERS, RADIAL, LATENT), RADIAL ** -0.5, 2.0, (), jnp.float32)
    w_edge = gaussian(keys[14], (MEMBERS, LATENT, LATENT), LATENT ** -0.5, 0.375, (), jnp.float32)
    w_out = gaussian(keys[15], (MEMBERS, LATENT), LATENT ** -0.5, 0.375, (), jnp.float32)
    return dict(positions=positions, velocities=velocities, species=species, counts=counts, neighbours=neighbours, send_lists=send_lists, inv_mass=inv_mass, w_rad_one=w_rad_one, emb_nbr=emb_nbr, emb_self=emb_self, w_one=w_one, w_src=w_src, w_dst=w_dst, w_rad_two=w_rad_two, w_edge=w_edge, w_out=w_out)


box_side = 4.0
soft_square = 0.25
centre_step = 0.75
basis_width = 0.75
pool_scale = 0.25
time_step = 0.25
highest = lax.Precision.HIGHEST

def radial_basis(distance):
    centres = centre_step * jnp.arange(RADIAL, dtype=jnp.float32)
    scaled = (distance[None, :] - centres[:, None]) / basis_width
    return jnp.exp(-scaled * scaled)

def edge_terms(ext_pos, neighbours, counts):
    slot_count, own_count = neighbours.shape
    flat_index = neighbours.reshape(-1)
    centre_pos = jnp.tile(ext_pos[:, :own_count], (1, slot_count))
    separation = ext_pos[:, flat_index] - centre_pos
    distance = jnp.sqrt(lax.optimization_barrier(jnp.sum(separation * separation, axis=0)) + soft_square)
    live_mask = (jnp.arange(slot_count, dtype=jnp.int32)[:, None] < counts[None, :]).astype(jnp.float32).reshape(-1)
    return (radial_basis(distance), live_mask, flat_index)

def first_layer(ext_pos, ext_onehot, neighbours, counts, w_rad_one, emb_nbr, emb_self, w_one):
    slot_count, own_count = neighbours.shape
    radial_terms, live_mask, flat_index = edge_terms(ext_pos, neighbours, counts)
    radial = jnp.einsum('mkl,ke->mle', w_rad_one, radial_terms, precision=highest)
    embedded = jnp.einsum('msl,se->mle', emb_nbr, ext_onehot[:, flat_index], precision=highest)
    members, latent = (radial.shape[0], radial.shape[1])
    pooled = (radial * embedded * live_mask).reshape(members, latent, slot_count, own_count).sum(axis=2) * pool_scale
    before = jnp.einsum('mkl,mka->mla', w_one, pooled, precision=highest)
    before = before + jnp.einsum('msl,sa->mla', emb_self, ext_onehot[:, :own_count], precision=highest)
    return jax.nn.silu(before)

def second_layer(hidden, ghost_feat, ext_pos, neighbours, counts, w_src, w_dst, w_rad_two, w_edge, w_out):
    slot_count = neighbours.shape[0]
    radial_terms, live_mask, flat_index = edge_terms(ext_pos, neighbours, counts)
    own_feat = jnp.einsum('mkl,mka->mla', w_dst, hidden, precision=highest)
    ext_feat = jnp.concatenate([own_feat, ghost_feat], axis=2)
    centre_feat = jnp.einsum('mkl,mka->mla', w_src, hidden, precision=highest)
    pair = jnp.tile(centre_feat, (1, 1, slot_count)) + ext_feat[:, :, flat_index]
    pair = jax.nn.silu(pair + jnp.einsum('mkl,ke->mle', w_rad_two, radial_terms, precision=highest))
    update = jax.nn.silu(jnp.einsum('mkl,mke->mle', w_edge, pair, precision=highest))
    pair_energy = jnp.einsum('ml,mle->e', w_out, update, precision=highest)
    return jnp.sum(pair_energy * live_mask) / w_out.shape[0]

def reference(positions, velocities, species, counts, neighbours, send_lists, inv_mass, w_rad_one, emb_nbr, emb_self, w_one, w_src, w_dst, w_rad_two, w_edge, w_out):
    boxes = N_GX * N_GY
    box_ids = jnp.arange(boxes, dtype=jnp.int32)
    row_a = box_ids // N_GY
    row_b = box_ids % N_GY
    left_x = (row_a + N_GX - 1) % N_GX * N_GY + row_b
    right_x = (row_a + 1) % N_GX * N_GY + row_b
    left_y = row_a * N_GY + (row_b + N_GY - 1) % N_GY
    right_y = row_a * N_GY + (row_b + 1) % N_GY
    lists = send_lists.reshape(4, boxes, GHOSTS)

    def picked(number, source):
        return lists[number][source] + source[:, None] * ATOMS_DEV
    ghost_index = jnp.stack([picked(2, left_x), picked(3, left_x), picked(0, right_x), picked(1, right_x), picked(1, left_y), picked(3, left_y), picked(0, right_y), picked(2, right_y)], axis=1)
    ghost_index = ghost_index.reshape(boxes, 8 * GHOSTS).astype(jnp.int32)
    sign_x = jnp.array([-1.0, -1.0, 1.0, 1.0, 0.0, 0.0, 0.0, 0.0], dtype=jnp.float32)
    sign_y = jnp.array([0.0, 0.0, 0.0, 0.0, -1.0, -1.0, 1.0, 1.0], dtype=jnp.float32)
    offsets = box_side * jnp.stack([jnp.repeat(sign_x, GHOSTS), jnp.repeat(sign_y, GHOSTS), jnp.zeros(8 * GHOSTS, jnp.float32)])
    ext_species = jnp.concatenate([species.reshape(boxes, ATOMS_DEV), species[ghost_index.reshape(-1)].reshape(boxes, 8 * GHOSTS)], axis=1)
    ext_onehot = (ext_species[:, None, :] == jnp.arange(SPECIES, dtype=jnp.int32)[None, :, None]).astype(jnp.float32)
    box_nbrs = neighbours.reshape(NEIGHBOURS, boxes, ATOMS_DEV).transpose(1, 0, 2)
    box_counts = counts.reshape(boxes, ATOMS_DEV)

    def energy(place):
        own = place.reshape(3, boxes, ATOMS_DEV).transpose(1, 0, 2)
        ghost = place[:, ghost_index.reshape(-1)].reshape(3, boxes, 8 * GHOSTS).transpose(1, 0, 2) + offsets[None]
        ext_all = jnp.concatenate([own, ghost], axis=2)

        def layer_one(inputs):
            return first_layer(inputs[0], inputs[1], inputs[2], inputs[3], w_rad_one, emb_nbr, emb_self, w_one)
        hidden_all = lax.map(jax.checkpoint(layer_one), (ext_all, ext_onehot, box_nbrs, box_counts))
        feat_all = jnp.einsum('mkl,dmka->dmla', w_dst, hidden_all, precision=highest)
        feat_glob = feat_all.transpose(1, 2, 0, 3).reshape(MEMBERS, LATENT, ATOMS)
        ghost_feat = feat_glob[:, :, ghost_index.reshape(-1)].reshape(MEMBERS, LATENT, boxes, 8 * GHOSTS).transpose(2, 0, 1, 3)

        def layer_two(inputs):
            return second_layer(inputs[0], inputs[1], inputs[2], inputs[3], inputs[4], w_src, w_dst, w_rad_two, w_edge, w_out)
        return jnp.sum(lax.map(jax.checkpoint(layer_two), (hidden_all, ghost_feat, ext_all, box_nbrs, box_counts)))
    forces = -jax.grad(energy)(positions)
    own_onehot = (species[None, :] == jnp.arange(SPECIES, dtype=jnp.int32)[:, None]).astype(jnp.float32)
    inv_scale = lax.optimization_barrier(jnp.sum(own_onehot * inv_mass[:, None], axis=0))
    new_velocities = velocities + time_step * inv_scale[None, :] * forces
    new_positions = positions + time_step * new_velocities
    return (new_positions, new_velocities)
```

```python
import jax
import jax.numpy as jnp
from jax import lax
from jax.experimental import pallas as pl
from jax.experimental.pallas import tpu as pltpu
from jax.sharding import PartitionSpec as P

SPECIES = 4
RADIAL = 8
FEATS = 40
OWN = 128
SLOTS = 12
EXT = 640
EDGES = SLOTS * OWN
LATENT = 256
MEMBERS = 4
STEP = 512

box_side = 4.0
soft_square = 0.25
centre_step = 0.75
basis_width = 0.75
pool_scale = 0.25
time_step = 0.25

f32 = jnp.float32
bf16 = jnp.bfloat16
NT = (((1,), (1,)), ((), ()))


def vmem(count):
    return [pl.BlockSpec(memory_space=pltpu.VMEM)] * count


def params():
    return pltpu.CompilerParams(vmem_limit_bytes=56 * 1024 * 1024)


def mm(a, b):
    return jnp.dot(a, b, preferred_element_type=f32)


def mm_nt(a, b):
    return lax.dot_general(a, b, NT, preferred_element_type=f32)


def split2(x):
    hi = x.astype(bf16)
    lo = (x - hi.astype(f32)).astype(bf16)
    return hi, lo


def split3(x):
    one = x.astype(bf16).astype(f32)
    rest = x - one
    two = rest.astype(bf16).astype(f32)
    return one, two, rest - two


def stacked3(x, rows):
    parts = list(split3(x))
    left = rows - 3 * x.shape[0]
    if left:
        parts.append(jnp.zeros((left, x.shape[1]), f32))
    return jnp.concatenate(parts, axis=0).astype(bf16)


def unstacked3(x, rows):
    return x[0:rows] + x[rows : 2 * rows] + x[2 * rows : 3 * rows]


def one_hot(rows, index_row, first=0):
    ids = lax.broadcasted_iota(jnp.int32, (rows, index_row.shape[1]), 0) + first
    return (ids == index_row).astype(f32).astype(bf16)


def lists_of(send_ref):
    pairs = ((2, 3), (0, 1), (1, 3), (0, 2))
    return [
        jnp.concatenate([send_ref[a : a + 1, :], send_ref[b : b + 1, :]], axis=1) for a, b in pairs
    ]


def pack_kernel(pos_ref, spec_ref, send_ref, own_ref, o0, o1, o2, o3):
    own = jnp.concatenate(
        [pos_ref[...], spec_ref[...].astype(f32), jnp.zeros((4, OWN), f32)], axis=0
    )
    own_ref[...] = own
    stacked = stacked3(own, 32)
    for out, index in zip((o0, o1, o2, o3), lists_of(send_ref)):
        out[...] = unstacked3(mm(stacked, one_hot(OWN, index)), 8)


def prep_kernel(
    nbr_ref,
    counts_ref,
    wr1_ref,
    nbr_emb_ref,
    self_emb_ref,
    wone_ref,
    wsrc_ref,
    wdst_ref,
    wr2_ref,
    wedge_ref,
    wout_ref,
    a_ref,
    at_ref,
    live_ref,
    weff_ref,
    wback_ref,
    wr2s_ref,
    wr2b_ref,
    src_ref,
    dst_ref,
    edge_ref,
    eout_ref,
):
    slot_ids = lax.broadcasted_iota(jnp.int32, (SLOTS, OWN), 0)
    live = slot_ids < counts_ref[...]
    live_ref[...] = live.astype(f32)
    masked = jnp.where(live, nbr_ref[...], -1)
    padded = jnp.concatenate([masked, jnp.full((OWN - SLOTS, OWN), -1, jnp.int32)], axis=0)
    columns = jnp.transpose(padded)
    lanes = lax.broadcasted_iota(jnp.int32, (OWN, EXT), 1)
    centre = lax.broadcasted_iota(jnp.int32, (OWN, OWN), 0)
    atom = lax.broadcasted_iota(jnp.int32, (1, OWN), 1)
    for s in range(SLOTS):
        a_ref[s * OWN : (s + 1) * OWN, :] = (lanes == columns[:, s : s + 1]).astype(f32).astype(bf16)
        row = masked[s : s + 1, :]
        at_ref[0:EXT, s * OWN : (s + 1) * OWN] = one_hot(EXT, row)
        own_row = jnp.where(row >= 0, atom, -1)
        at_ref[EXT : EXT + OWN, s * OWN : (s + 1) * OWN] = (
            (centre == own_row).astype(f32).astype(bf16)
        )
    for m in range(MEMBERS):
        mixed = jnp.concatenate(
            [wr1_ref[m] * nbr_emb_ref[m, sp : sp + 1, :] for sp in range(SPECIES)], axis=0
        )
        eff = pool_scale * jnp.dot(
            mixed, wone_ref[m], precision=lax.Precision.HIGHEST, preferred_element_type=f32
        )
        full = jnp.concatenate([eff, self_emb_ref[m], jnp.zeros((4, LATENT), f32)], axis=0)
        hi = full.astype(bf16).astype(f32)
        lo = full - hi
        weff_ref[m] = jnp.concatenate([hi, hi, lo, jnp.zeros((8, LATENT), f32)], axis=0).astype(bf16)
        hi, lo = hi[0:32], lo[0:32]
        wback_ref[m, 0] = jnp.concatenate([hi, lo, jnp.zeros((64, LATENT), f32)], axis=0).astype(bf16)
        wback_ref[m, 1] = jnp.concatenate([hi, jnp.zeros((96, LATENT), f32)], axis=0).astype(bf16)
        full = wr2_ref[m]
        hi = full.astype(bf16).astype(f32)
        lo = full - hi
        wr2s_ref[m] = jnp.concatenate([hi, hi, lo, jnp.zeros((104, LATENT), f32)], axis=0).astype(
            bf16
        )
        wr2b_ref[m, 0] = jnp.concatenate([hi, lo, jnp.zeros((112, LATENT), f32)], axis=0).astype(bf16)
        wr2b_ref[m, 1] = jnp.concatenate([hi, jnp.zeros((120, LATENT), f32)], axis=0).astype(bf16)
        for given, kept in ((wsrc_ref, src_ref), (wdst_ref, dst_ref), (wedge_ref, edge_ref)):
            hi, lo = split2(given[m])
            kept[m, 0] = hi
            kept[m, 1] = lo
        hi, lo = split2(wedge_ref[m] * (wout_ref[m : m + 1, :] * (1.0 / MEMBERS)))
        eout_ref[m, 0] = hi
        eout_ref[m, 1] = lo


def geometry_kernel(own_ref, g0, g1, g2, g3, send_ref, at_ref, live_ref, b_ref, geo_ref, basis_ref, o0, o1, o2, o3):
    own = own_ref[...]
    rows = lax.broadcasted_iota(jnp.int32, (8, OWN), 0)
    pieces = [own]
    for ref, row, by in ((g0, 0, -box_side), (g1, 0, box_side), (g2, 1, -box_side), (g3, 1, box_side)):
        pieces.append(ref[...] + jnp.where(rows == row, by, 0.0))
    ext = jnp.concatenate(pieces, axis=1)
    there = unstacked3(mm(stacked3(ext, 32), at_ref[0:EXT, :]), 8)
    centres = centre_step * lax.broadcasted_iota(jnp.int32, (RADIAL, OWN), 0).astype(f32)
    sums = [jnp.zeros((RADIAL, OWN), f32) for _ in range(SPECIES)]
    for s in range(SLOTS):
        other = there[:, s * OWN : (s + 1) * OWN]
        sep = other - own
        square = sep[0:1] * sep[0:1] + sep[1:2] * sep[1:2] + sep[2:3] * sep[2:3]
        distance = jnp.sqrt(square + soft_square)
        scaled = (distance - centres) / basis_width
        basis = jnp.exp(-scaled * scaled)
        basis_ref[:, s * OWN : (s + 1) * OWN] = basis
        geo_ref[:, s * OWN : (s + 1) * OWN] = jnp.where(
            rows == 4, distance, jnp.where(rows < 3, sep, other)
        )
        kind = other[3:4]
        alive = live_ref[s : s + 1, :]
        for sp in range(SPECIES):
            sums[sp] = sums[sp] + basis * jnp.where(kind == float(sp), alive, 0.0)
    flags = jnp.where(rows.astype(f32) == own[3:4], 1.0, 0.0)
    b_own = jnp.concatenate(sums + [flags], axis=0)
    b_ref[...] = b_own
    stacked = stacked3(b_own, OWN)
    for out, index in zip((o0, o1, o2, o3), lists_of(send_ref)):
        out[...] = unstacked3(mm(stacked, one_hot(OWN, index)), FEATS)


def half_tanh(x):
    return 0.5 + 0.5 * jnp.tanh(0.5 * x)


def main_kernel(
    b0,
    b1,
    b2,
    b3,
    b4,
    basis_ref,
    a_ref,
    at_ref,
    weff_ref,
    wback_ref,
    wr2s_ref,
    wr2b_ref,
    src_ref,
    dst_ref,
    edge_ref,
    eout_ref,
    c0,
    c1,
    c2,
    c3,
    c4,
    ctb_out,
    xb,
    bs,
    slope,
    u_hi,
    u_lo,
    centre,
    cx_hi,
    cx_lo,
    ctb,
    acc,
):
    for n, ref in enumerate((b0, b1, b2, b3, b4)):
        full = ref[...]
        hi = full.astype(bf16).astype(f32)
        lo = full - hi
        tall = jnp.concatenate([hi, lo, hi, jnp.zeros((8, OWN), f32)], axis=0)
        xb[n * OWN : (n + 1) * OWN, :] = jnp.transpose(tall).astype(bf16)
    for s in range(SLOTS):
        full = basis_ref[:, s * OWN : (s + 1) * OWN]
        hi = full.astype(bf16).astype(f32)
        lo = full - hi
        tall = jnp.concatenate([hi, lo, hi, jnp.zeros((104, OWN), f32)], axis=0)
        bs[s * OWN : (s + 1) * OWN, :] = jnp.transpose(tall).astype(bf16)
    ctb[...] = jnp.zeros_like(ctb)
    acc[...] = jnp.zeros_like(acc)

    def three(dot, hi, lo, w_ref, m):
        return dot(hi, w_ref[m, 0]) + dot(lo, w_ref[m, 0]) + dot(hi, w_ref[m, 1])

    @pl.loop(0, MEMBERS)
    def _(m):
        pre = mm(xb[...], weff_ref[m])
        sig = half_tanh(pre)
        hid = pre * sig
        slope[...] = sig + hid * (1.0 - sig)
        hi, lo = split2(hid)
        hi2, lo2 = split2(three(mm, hi, lo, dst_ref, m))
        u_hi[...] = hi2
        u_lo[...] = lo2
        centre[...] = three(mm, hi[0:OWN], lo[0:OWN], src_ref, m)

        @pl.loop(0, EDGES // STEP)
        def _(t):
            at = pl.ds(pl.multiple_of(t * STEP, STEP), STEP)
            pick = a_ref[at, :]
            x = mm(pick, u_hi[...]) + mm(pick, u_lo[...]) + mm(bs[at, :], wr2s_ref[m])
            x = x + jnp.concatenate([centre[...]] * (STEP // OWN), axis=0)
            sig = half_tanh(x)
            pair = x * sig
            dx = sig + pair * (1.0 - sig)
            hi, lo = split2(pair)
            y = three(mm, hi, lo, edge_ref, m)
            sig = half_tanh(y)
            hi, lo = split2(sig + y * sig * (1.0 - sig))
            hi, lo = split2(three(mm_nt, hi, lo, eout_ref, m) * dx)
            cx_hi[at, :] = hi
            cx_lo[at, :] = lo
            ctb[at, :] += mm_nt(hi, wr2b_ref[m, 0]) + mm_nt(lo, wr2b_ref[m, 1])

        ct = mm(at_ref[...], cx_hi[...]) + mm(at_ref[...], cx_lo[...])
        hi, lo = split2(ct)
        ct_hid = three(mm_nt, hi[0:EXT], lo[0:EXT], dst_ref, m)
        ct_own = three(mm_nt, hi[EXT:], lo[EXT:], src_ref, m)
        ct_hid = jnp.concatenate([ct_hid[0:OWN] + ct_own, ct_hid[OWN:]], axis=0)
        hi, lo = split2(ct_hid * slope[...])
        acc[...] += mm_nt(hi, wback_ref[m, 0]) + mm_nt(lo, wback_ref[m, 1])

    for n, ref in enumerate((c0, c1, c2, c3, c4)):
        wide = jnp.transpose(acc[n * OWN : (n + 1) * OWN, :])
        ref[...] = wide[0:32] + wide[32:64]
    for s in range(SLOTS):
        wide = jnp.transpose(ctb[s * OWN : (s + 1) * OWN, :])
        ctb_out[:, s * OWN : (s + 1) * OWN] = wide[0:8] + wide[8:16]


def list_columns(send_ref):
    pairs = ((0, 1), (2, 3), (0, 2), (1, 3))
    return [
        jnp.concatenate([send_ref[a : a + 1, :], send_ref[b : b + 1, :]], axis=1) for a, b in pairs
    ]


def collected(pieces, send_ref, rows):
    total = None
    for piece, index in zip(pieces, list_columns(send_ref)):
        got = unstacked3(
            mm_nt(stacked3(piece[...], -(-3 * rows // 16) * 16), one_hot(OWN, index)), rows
        )
        total = got if total is None else total + got
    return total


def push_kernel(own_ct, r0, r1, r2, r3, send_ref, basis_ref, geo_ref, live_ref, ctb_ref, a_ref, own_out, o0, o1, o2, o3):
    ct = own_ct[...] + collected((r0, r1, r2, r3), send_ref, 32)
    rows = lax.broadcasted_iota(jnp.int32, (8, OWN), 0)
    centres = centre_step * lax.broadcasted_iota(jnp.int32, (RADIAL, OWN), 0).astype(f32)
    pulled = jnp.zeros((8, OWN), f32)
    seps = []
    for s in range(SLOTS):
        at = slice(s * OWN, (s + 1) * OWN)
        geo = geo_ref[:, at]
        kind = geo[3:4]
        picked = ctb_ref[:, at]
        for sp in range(SPECIES):
            picked = picked + jnp.where(kind == float(sp), ct[sp * 8 : sp * 8 + 8], 0.0)
        distance = geo[4:5]
        slope = picked * basis_ref[:, at] * (distance - centres)
        ct_d = jnp.sum(slope, axis=0, keepdims=True) * (-2.0 / (basis_width * basis_width))
        ct_sep = jnp.where(rows < 3, geo * (ct_d * live_ref[s : s + 1, :] / distance), 0.0)
        pulled = pulled - ct_sep
        seps.append(ct_sep)
    all_sep = jnp.concatenate(seps, axis=1)
    spread = unstacked3(mm(stacked3(all_sep, 32), a_ref[...]), 8)
    own_out[...] = spread[:, 0:OWN] + pulled
    for n, out in enumerate((o0, o1, o2, o3)):
        out[...] = spread[:, (n + 1) * OWN : (n + 2) * OWN]


def finish_kernel(own_ct, r0, r1, r2, r3, send_ref, pos_ref, vel_ref, spec_ref, mass_ref, pos_out, vel_out):
    ct = own_ct[...] + collected((r0, r1, r2, r3), send_ref, 8)
    spec = spec_ref[...]
    scale = jnp.zeros(spec.shape, f32)
    for sp in range(SPECIES):
        scale = scale + jnp.where(spec == sp, mass_ref[sp], 0.0)
    vel = vel_ref[...] - time_step * scale * ct[0:3]
    vel_out[...] = vel
    pos_out[...] = pos_ref[...] + time_step * vel


def shifted(shard, axis, by):
    peers = lax.axis_size(axis)
    return lax.ppermute(shard, axis, [(i, (i + by) % peers) for i in range(peers)])


def sent(four):
    return (
        shifted(four[0], "gx", 1),
        shifted(four[1], "gx", -1),
        shifted(four[2], "gy", 1),
        shifted(four[3], "gy", -1),
    )


def returned(four):
    return (
        shifted(four[1], "gx", 1),
        shifted(four[0], "gx", -1),
        shifted(four[3], "gy", 1),
        shifted(four[2], "gy", -1),
    )


def like(*shape):
    return jax.ShapeDtypeStruct(shape, f32)


def like16(*shape):
    return jax.ShapeDtypeStruct(shape, bf16)


def shards(
    positions,
    velocities,
    species,
    counts,
    neighbours,
    send_lists,
    inv_mass,
    w_rad_one,
    emb_nbr,
    emb_self,
    w_one,
    w_src,
    w_dst,
    w_rad_two,
    w_edge,
    w_out,
):
    spec = species[None, :]
    own, *packed = pl.pallas_call(
        pack_kernel,
        out_shape=[like(8, OWN)] * 5,
        in_specs=vmem(3),
        out_specs=vmem(5),
        name="pack",
    )(positions, spec, send_lists)
    ghosts = sent(packed)
    a, at, live, weff, wback, wr2s, wr2b, src, dst, edge, eout = pl.pallas_call(
        prep_kernel,
        out_shape=[
            like16(EDGES, EXT),
            like16(EXT + OWN, EDGES),
            like(SLOTS, OWN),
            like16(MEMBERS, 128, LATENT),
            like16(MEMBERS, 2, 128, LATENT),
            like16(MEMBERS, 128, LATENT),
            like16(MEMBERS, 2, 128, LATENT),
        ]
        + [like16(MEMBERS, 2, LATENT, LATENT)] * 4,
        in_specs=vmem(11),
        out_specs=vmem(11),
        compiler_params=params(),
        cost_estimate=pl.CostEstimate(flops=200_000_000, bytes_accessed=16_000_000, transcendentals=0),
        name="prep",
    )(
        neighbours,
        counts[None, :],
        w_rad_one,
        emb_nbr,
        emb_self,
        w_one,
        w_src,
        w_dst,
        w_rad_two,
        w_edge,
        w_out,
    )
    b_own, geo, basis, *b_packed = pl.pallas_call(
        geometry_kernel,
        out_shape=[like(FEATS, OWN), like(8, EDGES), like(8, EDGES)] + [like(FEATS, OWN)] * 4,
        in_specs=vmem(8),
        out_specs=vmem(7),
        compiler_params=params(),
        name="geometry",
    )(own, *ghosts, send_lists, at, live)
    b_ghosts = sent(b_packed)
    *cts, ctb = pl.pallas_call(
        main_kernel,
        out_shape=[like(32, OWN)] * 5 + [like(8, EDGES)],
        in_specs=vmem(16),
        out_specs=vmem(6),
        scratch_shapes=[
            pltpu.VMEM((EXT, 128), bf16),
            pltpu.VMEM((EDGES, 128), bf16),
            pltpu.VMEM((EXT, LATENT), f32),
            pltpu.VMEM((EXT, LATENT), bf16),
            pltpu.VMEM((EXT, LATENT), bf16),
            pltpu.VMEM((OWN, LATENT), f32),
            pltpu.VMEM((EDGES, LATENT), bf16),
            pltpu.VMEM((EDGES, LATENT), bf16),
            pltpu.VMEM((EDGES, 128), f32),
            pltpu.VMEM((EXT, 128), f32),
        ],
        compiler_params=params(),
        name="members",
    )(b_own, *b_ghosts, basis, a, at, weff, wback, wr2s, wr2b, src, dst, edge, eout)
    back = returned(cts[1:])
    own_ct, *outgoing = pl.pallas_call(
        push_kernel,
        out_shape=[like(8, OWN)] * 5,
        in_specs=vmem(11),
        out_specs=vmem(5),
        compiler_params=params(),
        name="push",
    )(cts[0], *back, send_lists, basis, geo, live, ctb, a)
    last = returned(outgoing)
    new_positions, new_velocities = pl.pallas_call(
        finish_kernel,
        out_shape=[like(3, OWN), like(3, OWN)],
        in_specs=vmem(9) + [pl.BlockSpec(memory_space=pltpu.SMEM)],
        out_specs=vmem(2),
        name="finish",
    )(own_ct, *last, send_lists, positions, velocities, spec, inv_mass)
    return (new_positions, new_velocities)


def solution(mesh):
    split = P(None, ("gx", "gy"))
    row = P(("gx", "gy"))
    placed = (split, split, row, row, split, split) + (P(),) * 10
    return jax.shard_map(
        shards, mesh=mesh, in_specs=placed, out_specs=(split, split), check_vma=False
    )
```

```python
import jax
import jax.numpy as jnp
from jax import lax
from jax.experimental import pallas as pl
from jax.experimental.pallas import tpu as pltpu
from jax.sharding import PartitionSpec as P

SPECIES = 4
RADIAL = 8
FEATS = 40
OWN = 128
SLOTS = 12
EXT = 640
EDGES = SLOTS * OWN
LATENT = 256
MEMBERS = 4
STEP = 256
LAG = 1

box_side = 4.0
soft_square = 0.25
centre_step = 0.75
basis_width = 0.75
pool_scale = 0.25
time_step = 0.25

f32 = jnp.float32
bf16 = jnp.bfloat16
NT = (((1,), (1,)), ((), ()))


def vmem(count):
    return [pl.BlockSpec(memory_space=pltpu.VMEM)] * count


def hbm(count):
    return [pl.BlockSpec(memory_space=pltpu.HBM)] * count


def params(mib):
    return pltpu.CompilerParams(vmem_limit_bytes=mib * 1024 * 1024)


def mm(a, b):
    return jnp.dot(a, b, preferred_element_type=f32)


def mm_nt(a, b):
    return lax.dot_general(a, b, NT, preferred_element_type=f32)


def split2(x):
    hi = x.astype(bf16)
    lo = (x - hi.astype(f32)).astype(bf16)
    return hi, lo


def split3(x):
    one = x.astype(bf16).astype(f32)
    rest = x - one
    two = rest.astype(bf16).astype(f32)
    return one, two, rest - two


def stacked3(x, rows):
    parts = list(split3(x))
    left = rows - 3 * x.shape[0]
    if left:
        parts.append(jnp.zeros((left, x.shape[1]), f32))
    return jnp.concatenate(parts, axis=0).astype(bf16)


def unstacked3(x, rows):
    return x[0:rows] + x[rows : 2 * rows] + x[2 * rows : 3 * rows]


def one_hot(rows, index_row, first=0):
    ids = lax.broadcasted_iota(jnp.int32, (rows, index_row.shape[1]), 0) + first
    return (ids == index_row).astype(f32).astype(bf16)


def lists_of(send_ref):
    pairs = ((2, 3), (0, 1), (1, 3), (0, 2))
    return [
        jnp.concatenate([send_ref[a : a + 1, :], send_ref[b : b + 1, :]], axis=1) for a, b in pairs
    ]


def odd_along(axis):
    return lax.rem(lax.axis_index(axis), 2) == 1


def by_partner(plus_x, minus_x, plus_y, minus_y):
    odd_x, odd_y = odd_along("gx"), odd_along("gy")
    return (
        jnp.where(odd_x, plus_x, minus_x),
        jnp.where(odd_x, minus_x, plus_x),
        jnp.where(odd_y, plus_y, minus_y),
        jnp.where(odd_y, minus_y, plus_y),
    )


def by_side(refs):
    s0, s1, s2, s3 = [ref[...] for ref in refs]
    odd_x, odd_y = odd_along("gx"), odd_along("gy")
    return (
        jnp.where(odd_x, s0, s1),
        jnp.where(odd_x, s1, s0),
        jnp.where(odd_y, s2, s3),
        jnp.where(odd_y, s3, s2),
    )


def fetched(given, kept, sems):
    copies = []
    for n, (source, target) in enumerate(zip(given, kept)):
        copies.append(pltpu.make_async_copy(source, target, sems.at[n]))
        copies[-1].start()
    return copies


def pack_kernel(pos_hbm, spec_hbm, send_hbm, own_ref, o0, o1, o2, o3, pos_ref, spec_ref, send_ref, sems):
    for copy in fetched((pos_hbm, spec_hbm, send_hbm), (pos_ref, spec_ref, send_ref), sems):
        copy.wait()
    own = jnp.concatenate(
        [pos_ref[...], spec_ref[...].astype(f32), jnp.zeros((4, OWN), f32)], axis=0
    )
    own_ref[...] = own
    stacked = stacked3(own, 32)
    for out, index in zip((o0, o1, o2, o3), by_partner(*lists_of(send_ref))):
        out[...] = unstacked3(mm(stacked, one_hot(OWN, index)), 8)


def halves(full):
    hi = full.astype(bf16).astype(f32)
    return hi, full - hi


def padded_rows(parts, rows):
    left = rows - sum(part.shape[0] for part in parts)
    return jnp.concatenate(parts + [jnp.zeros((left, parts[0].shape[1]), f32)], axis=0).astype(bf16)


def stack_rows(ref, m, full):
    hi, lo = split2(full)
    ref[m, 0:LATENT] = hi
    ref[m, LATENT : 2 * LATENT] = hi
    ref[m, 2 * LATENT : 3 * LATENT] = lo


def stack_columns(ref, m, full):
    hi, lo = split2(full)
    ref[m, :, 0:LATENT] = hi
    ref[m, :, LATENT : 2 * LATENT] = hi
    ref[m, :, 2 * LATENT :] = lo


def picks_kernel(nbr_hbm, counts_hbm, a_ref, at_ref, live_ref, alive_ref, nbr_ref, counts_ref, sems):
    for copy in fetched((nbr_hbm, counts_hbm), (nbr_ref, counts_ref), sems):
        copy.wait()
    slot_ids = lax.broadcasted_iota(jnp.int32, (SLOTS, OWN), 0)
    live = (slot_ids < counts_ref[...]).astype(f32)
    live_ref[...] = live
    nbr = nbr_ref[...]
    rest = OWN - SLOTS
    columns = jnp.transpose(jnp.concatenate([nbr, jnp.zeros((rest, OWN), jnp.int32)], axis=0))
    alive = jnp.transpose(jnp.concatenate([live, jnp.zeros((rest, OWN), f32)], axis=0))
    lanes = lax.broadcasted_iota(jnp.int32, (OWN, EXT), 1)
    for s in range(SLOTS):
        at = slice(s * OWN, (s + 1) * OWN)
        a_ref[at, :] = (lanes == columns[:, s : s + 1]).astype(f32).astype(bf16)
        at_ref[:, at] = one_hot(EXT, nbr[s : s + 1, :])
        alive_ref[at, :] = jnp.broadcast_to(alive[:, s : s + 1], (OWN, OWN))


def weights_kernel(
    after_hbm,
    wr1_hbm,
    nbr_emb_hbm,
    self_emb_hbm,
    wr2_hbm,
    wout_hbm,
    wone_hbm,
    wsrc_hbm,
    wdst_hbm,
    wedge_hbm,
    weff_ref,
    wback_ref,
    wr2b_ref,
    src_ref,
    dst_ref,
    edge_ref,
    srct_ref,
    dstt_ref,
    eout_ref,
    wr1_ref,
    nbr_emb_ref,
    self_emb_ref,
    wr2_ref,
    wout_ref,
    wone_ref,
    wsrc_ref,
    wdst_ref,
    wedge_ref,
    sems,
    large_sems,
):
    small = fetched(
        (wr1_hbm, nbr_emb_hbm, self_emb_hbm, wr2_hbm, wout_hbm),
        (wr1_ref, nbr_emb_ref, self_emb_ref, wr2_ref, wout_ref),
        sems,
    )
    large = fetched(
        (wone_hbm, wsrc_hbm, wdst_hbm, wedge_hbm), (wone_ref, wsrc_ref, wdst_ref, wedge_ref), large_sems
    )
    for copy in small:
        copy.wait()
    large[0].wait()
    for m in range(MEMBERS):
        mixed = jnp.concatenate(
            [wr1_ref[m] * nbr_emb_ref[m, sp : sp + 1, :] for sp in range(SPECIES)], axis=0
        )
        eff = pool_scale * jnp.dot(
            mixed, wone_ref[m], precision=lax.Precision.HIGHEST, preferred_element_type=f32
        )
        full = 0.5 * jnp.concatenate([eff, self_emb_ref[m], jnp.zeros((4, LATENT), f32)], axis=0)
        hi, lo = halves(full)
        weff_ref[m] = padded_rows([hi, hi, lo], 128)
        hi, lo = hi[0:32], lo[0:32]
        wback_ref[m, :, 0:LATENT] = padded_rows([hi, lo], 128)
        wback_ref[m, :, LATENT:] = padded_rows([hi], 128)
        hi, lo = halves(wr2_ref[m])
        dst_ref[m, 3 * LATENT :] = padded_rows([0.5 * hi, 0.5 * hi, 0.5 * lo], 128)
        wr2b_ref[m, :, 0:LATENT] = padded_rows([hi, lo], 128)
        wr2b_ref[m, :, LATENT:] = padded_rows([hi], 128)
    large[1].wait()
    for m in range(MEMBERS):
        stack_rows(src_ref, m, 0.5 * wsrc_ref[m])
        stack_columns(srct_ref, m, wsrc_ref[m])
    large[2].wait()
    for m in range(MEMBERS):
        stack_rows(dst_ref, m, 0.5 * wdst_ref[m])
        stack_columns(dstt_ref, m, wdst_ref[m])
    large[3].wait()
    for m in range(MEMBERS):
        readout = wout_ref[m : m + 1, :] * (0.25 / MEMBERS)
        stack_rows(edge_ref, m, 0.5 * wedge_ref[m])
        stack_columns(eout_ref, m, wedge_ref[m] * readout)


def geometry_kernel(own_ref, g0, g1, g2, g3, send_ref, at_ref, live_ref, b_ref, geo_ref, basis_ref, o0, o1, o2, o3):
    own = own_ref[...]
    rows = lax.broadcasted_iota(jnp.int32, (8, OWN), 0)
    pieces = [own]
    px, mx, py, my = by_side((g0, g1, g2, g3))
    for piece, row, by in ((mx, 0, -box_side), (px, 0, box_side), (my, 1, -box_side), (py, 1, box_side)):
        pieces.append(piece + jnp.where(rows == row, by, 0.0))
    ext = jnp.concatenate(pieces, axis=1)
    there = unstacked3(mm(stacked3(ext, 32), at_ref[...]), 8)
    centres = centre_step * lax.broadcasted_iota(jnp.int32, (RADIAL, OWN), 0).astype(f32)
    sums = [jnp.zeros((RADIAL, OWN), f32) for _ in range(SPECIES)]
    for s in range(SLOTS):
        other = there[:, s * OWN : (s + 1) * OWN]
        sep = other - own
        square = sep[0:1] * sep[0:1] + sep[1:2] * sep[1:2] + sep[2:3] * sep[2:3]
        distance = jnp.sqrt(square + soft_square)
        scaled = (distance - centres) / basis_width
        basis = jnp.exp(-scaled * scaled)
        basis_ref[:, s * OWN : (s + 1) * OWN] = basis
        geo_ref[:, s * OWN : (s + 1) * OWN] = jnp.where(
            rows == 4, distance, jnp.where(rows < 3, sep, other)
        )
        kind = other[3:4]
        alive = live_ref[s : s + 1, :]
        for sp in range(SPECIES):
            sums[sp] = sums[sp] + basis * jnp.where(kind == float(sp), alive, 0.0)
    flags = jnp.where(rows.astype(f32) == own[3:4], 1.0, 0.0)
    b_own = jnp.concatenate(sums + [flags], axis=0)
    b_ref[...] = b_own
    stacked = stacked3(b_own, OWN)
    for out, index in zip((o0, o1, o2, o3), by_partner(*lists_of(send_ref))):
        out[...] = unstacked3(mm(stacked, one_hot(OWN, index)), FEATS)


def silu_parts(half):
    above = 1.0 + jnp.tanh(half)
    value = half * above
    return value, above + value * (2.0 - above)


def tripled(x):
    hi, lo = split2(x)
    return jnp.concatenate([hi, lo, hi], axis=1)


def main_kernel(
    b0,
    b1,
    b2,
    b3,
    b4,
    basis_ref,
    a_ref,
    alive_ref,
    weff_ref,
    wback_ref,
    wr2b_ref,
    src_ref,
    dst_ref,
    edge_ref,
    srct_ref,
    dstt_ref,
    eout_ref,
    c0,
    c1,
    c2,
    c3,
    c4,
    ctb_out,
    xb,
    xe,
    bs,
    ctb,
    acc,
    acc_own,
):
    px, mx, py, my = by_side((b1, b2, b3, b4))
    for n, full in enumerate((b0[...], mx, px, my, py)):
        hi, lo = halves(full)
        tall = jnp.concatenate([hi, lo, hi, jnp.zeros((8, OWN), f32)], axis=0)
        xb[n * OWN : (n + 1) * OWN, :] = jnp.transpose(tall).astype(bf16)
    for s in range(SLOTS):
        hi, lo = halves(basis_ref[:, s * OWN : (s + 1) * OWN])
        tall = jnp.concatenate([hi, lo, hi, jnp.zeros((104, OWN), f32)], axis=0)
        bs[s * OWN : (s + 1) * OWN, :] = jnp.transpose(tall).astype(bf16)
    xe[...] = mm(a_ref[...], xb[...]).astype(bf16)
    ctb[...] = jnp.zeros_like(ctb)
    acc[...] = jnp.zeros_like(acc)
    acc_own[...] = jnp.zeros_like(acc_own)

    for m in range(MEMBERS):
        own_hid, own_slope = silu_parts(mm(xb[0:OWN, :], weff_ref[m]))
        centre = mm(tripled(own_hid), src_ref[m])
        many = jnp.concatenate([centre] * (STEP // OWN), axis=0)

        def rows_of(t):
            return slice(t * STEP, (t + 1) * STEP)

        def hidden(t, v):
            v["z"] = mm(xe[rows_of(t), :], weff_ref[m])

        def hidden_parts(t, v):
            hid, v["slope"] = silu_parts(v["z"])
            v["wide"] = tripled(hid)

        def pair(t, v):
            v["z"] = mm(v["wide"], dst_ref[m, 0 : 3 * LATENT]) + mm(bs[rows_of(t), :], dst_ref[m, 3 * LATENT :])

        def pair_parts(t, v):
            value, v["dx"] = silu_parts(v["z"] + many)
            v["wide"] = tripled(value)

        def update(t, v):
            v["z"] = mm(v["wide"], edge_ref[m])

        def update_parts(t, v):
            mask = alive_ref[rows_of(t), :]
            v["wide"] = tripled(silu_parts(v["z"])[1] * jnp.concatenate([mask, mask], axis=1))

        def pull_update(t, v):
            v["z"] = mm_nt(v["wide"], eout_ref[m])

        def pull_pair_parts(t, v):
            ct = v["z"] * v["dx"]
            v["sum"] = ct[0:OWN]
            for n in range(1, STEP // OWN):
                v["sum"] = v["sum"] + ct[n * OWN : (n + 1) * OWN]
            v["wide"] = tripled(ct)

        def pull_pair(t, v):
            ctb[rows_of(t), :] += mm_nt(v["wide"][:, 0 : 2 * LATENT], wr2b_ref[m])
            v["z"] = mm_nt(v["wide"], dstt_ref[m])

        def pull_hidden_parts(t, v):
            hi, lo = split2(v["z"] * v["slope"])
            v["wide"] = jnp.concatenate([hi, lo], axis=1)

        def pull_hidden(t, v):
            acc[rows_of(t), :] += mm_nt(v["wide"], wback_ref[m])

        stages = (
            hidden,
            hidden_parts,
            pair,
            pair_parts,
            update,
            update_parts,
            pull_update,
            pull_pair_parts,
            pull_pair,
            pull_hidden_parts,
            pull_hidden,
        )
        tiles = EDGES // STEP
        held = [{} for _ in range(tiles)]
        for tick in range((tiles - 1) * LAG + len(stages)):
            for t in range(tiles):
                stage = tick - t * LAG
                if 0 <= stage < len(stages):
                    stages[stage](t, held[t])
        total = held[0]["sum"]
        for t in range(1, tiles):
            total = total + held[t]["sum"]
        ct_own = mm_nt(tripled(total), srct_ref[m])
        hi, lo = split2(ct_own * own_slope)
        acc_own[...] += mm_nt(jnp.concatenate([hi, lo], axis=1), wback_ref[m])

    tall = []
    for s in range(SLOTS):
        at = slice(s * OWN, (s + 1) * OWN)
        wide = jnp.transpose(ctb[at, :])
        ctb_out[:, at] = wide[0:8] + wide[8:16]
        wide = jnp.transpose(acc[at, :])
        hi, lo = halves(wide[0:32] + wide[32:64])
        tall.append(jnp.concatenate([hi, lo], axis=0).astype(bf16))
    spread = mm(jnp.concatenate(tall, axis=1), a_ref[...])
    spread = spread[0:32] + spread[32:64]
    wide = jnp.transpose(acc_own[...])
    blocks = [spread[:, n * OWN : (n + 1) * OWN] for n in range(5)]
    c0[...] = blocks[0] + wide[0:32] + wide[32:64]
    for ref, block in zip((c1, c2, c3, c4), by_partner(blocks[2], blocks[1], blocks[4], blocks[3])):
        ref[...] = block


def collected(pieces, send_ref, rows):
    total = None
    for piece, index in zip(pieces, by_partner(*lists_of(send_ref))):
        got = unstacked3(
            mm_nt(stacked3(piece[...], -(-3 * rows // 16) * 16), one_hot(OWN, index)), rows
        )
        total = got if total is None else total + got
    return total


def push_kernel(own_ct, r0, r1, r2, r3, send_ref, basis_ref, geo_ref, live_ref, ctb_ref, a_ref, own_out, o0, o1, o2, o3):
    ct = own_ct[...] + collected((r0, r1, r2, r3), send_ref, 32)
    rows = lax.broadcasted_iota(jnp.int32, (8, OWN), 0)
    centres = centre_step * lax.broadcasted_iota(jnp.int32, (RADIAL, OWN), 0).astype(f32)
    pulled = jnp.zeros((8, OWN), f32)
    seps = []
    for s in range(SLOTS):
        at = slice(s * OWN, (s + 1) * OWN)
        geo = geo_ref[:, at]
        kind = geo[3:4]
        picked = ctb_ref[:, at]
        for sp in range(SPECIES):
            picked = picked + jnp.where(kind == float(sp), ct[sp * 8 : sp * 8 + 8], 0.0)
        distance = geo[4:5]
        slope = picked * basis_ref[:, at] * (distance - centres)
        ct_d = jnp.sum(slope, axis=0, keepdims=True) * (-2.0 / (basis_width * basis_width))
        ct_sep = jnp.where(rows < 3, geo * (ct_d * live_ref[s : s + 1, :] / distance), 0.0)
        pulled = pulled - ct_sep
        seps.append(ct_sep)
    all_sep = jnp.concatenate(seps, axis=1)
    spread = unstacked3(mm(stacked3(all_sep, 32), a_ref[...]), 8)
    own_out[...] = spread[:, 0:OWN] + pulled
    blocks = [spread[:, n * OWN : (n + 1) * OWN] for n in range(5)]
    for out, block in zip((o0, o1, o2, o3), by_partner(blocks[2], blocks[1], blocks[4], blocks[3])):
        out[...] = block


def finish_kernel(own_ct, r0, r1, r2, r3, send_ref, pos_ref, vel_ref, spec_ref, mass_ref, pos_out, vel_out):
    ct = own_ct[...] + collected((r0, r1, r2, r3), send_ref, 8)
    spec = spec_ref[...]
    scale = jnp.zeros(spec.shape, f32)
    for sp in range(SPECIES):
        scale = scale + jnp.where(spec == sp, mass_ref[sp], 0.0)
    vel = vel_ref[...] - time_step * scale * ct[0:3]
    vel_out[...] = vel
    pos_out[...] = pos_ref[...] + time_step * vel


def swapped(shard, axis, first):
    peers = lax.axis_size(axis)
    pairs = []
    for i in range(first, peers + first, 2):
        pairs += [(i % peers, (i + 1) % peers), ((i + 1) % peers, i % peers)]
    return lax.ppermute(shard, axis, pairs)


def exchanged(four):
    return (
        swapped(four[0], "gx", 1),
        swapped(four[1], "gx", 0),
        swapped(four[2], "gy", 1),
        swapped(four[3], "gy", 0),
    )


def like(*shape):
    return jax.ShapeDtypeStruct(shape, f32)


def like16(*shape):
    return jax.ShapeDtypeStruct(shape, bf16)


def run_picks(neighbours, counts):
    return pl.pallas_call(
        picks_kernel,
        out_shape=[
            like16(EDGES, EXT),
            like16(EXT, EDGES),
            like(SLOTS, OWN),
            like(EDGES, OWN),
        ],
        in_specs=hbm(2),
        out_specs=vmem(4),
        scratch_shapes=[
            pltpu.VMEM((SLOTS, OWN), jnp.int32),
            pltpu.VMEM((1, OWN), jnp.int32),
            pltpu.SemaphoreType.DMA((2,)),
        ],
        compiler_params=params(12),
        cost_estimate=pl.CostEstimate(flops=4_000_000_000, bytes_accessed=16_000_000, transcendentals=0),
        name="picks",
    )(neighbours, counts[None, :])


def run_weights(after, *given):
    return pl.pallas_call(
        weights_kernel,
        out_shape=[
            like16(MEMBERS, 128, LATENT),
            like16(MEMBERS, 128, 2 * LATENT),
            like16(MEMBERS, 128, 2 * LATENT),
            like16(MEMBERS, 3 * LATENT, LATENT),
            like16(MEMBERS, 3 * LATENT + 128, LATENT),
            like16(MEMBERS, 3 * LATENT, LATENT),
        ]
        + [like16(MEMBERS, LATENT, 3 * LATENT)] * 3,
        in_specs=hbm(10),
        out_specs=vmem(9),
        scratch_shapes=[
            pltpu.VMEM((MEMBERS, RADIAL, LATENT), f32),
            pltpu.VMEM((MEMBERS, SPECIES, LATENT), f32),
            pltpu.VMEM((MEMBERS, SPECIES, LATENT), f32),
            pltpu.VMEM((MEMBERS, RADIAL, LATENT), f32),
            pltpu.VMEM((MEMBERS, LATENT), f32),
        ]
        + [pltpu.VMEM((MEMBERS, LATENT, LATENT), f32)] * 4
        + [pltpu.SemaphoreType.DMA((5,)), pltpu.SemaphoreType.DMA((4,))],
        compiler_params=params(20),
        cost_estimate=pl.CostEstimate(flops=4_000_000_000, bytes_accessed=16_000_000, transcendentals=0),
        name="weights",
    )(after, *given)


def run_members(sums, basis, a, alive, weights):
    return pl.pallas_call(
        main_kernel,
        out_shape=[like(32, OWN)] * 5 + [like(8, EDGES)],
        in_specs=vmem(17),
        out_specs=vmem(6),
        scratch_shapes=[
            pltpu.VMEM((EXT, 128), bf16),
            pltpu.VMEM((EDGES, 128), bf16),
            pltpu.VMEM((EDGES, 128), bf16),
            pltpu.VMEM((EDGES, 128), f32),
            pltpu.VMEM((EDGES, 128), f32),
            pltpu.VMEM((OWN, 128), f32),
        ],
        compiler_params=params(40),
        name="members",
    )(*sums, basis, a, alive, *weights)


def shards(
    positions,
    velocities,
    species,
    counts,
    neighbours,
    send_lists,
    inv_mass,
    w_rad_one,
    emb_nbr,
    emb_self,
    w_one,
    w_src,
    w_dst,
    w_rad_two,
    w_edge,
    w_out,
):
    spec = species[None, :]
    own, *packed = pl.pallas_call(
        pack_kernel,
        out_shape=[like(8, OWN)] * 5,
        in_specs=hbm(3),
        out_specs=vmem(5),
        scratch_shapes=[
            pltpu.VMEM((3, OWN), f32),
            pltpu.VMEM((1, OWN), jnp.int32),
            pltpu.VMEM((4, OWN // 2), jnp.int32),
            pltpu.SemaphoreType.DMA((3,)),
        ],
        compiler_params=params(4),
        name="pack",
    )(positions, spec, send_lists)
    ghosts = exchanged(packed)
    a, at, live, alive = run_picks(neighbours, counts)
    b_own, geo, basis, *b_packed = pl.pallas_call(
        geometry_kernel,
        out_shape=[like(FEATS, OWN), like(8, EDGES), like(8, EDGES)] + [like(FEATS, OWN)] * 4,
        in_specs=vmem(8),
        out_specs=vmem(7),
        compiler_params=params(12),
        name="geometry",
    )(own, *ghosts, send_lists, at, live)
    b_ghosts = exchanged(b_packed)
    weights = run_weights(
        b_own, w_rad_one, emb_nbr, emb_self, w_rad_two, w_out, w_one, w_src, w_dst, w_edge
    )
    *cts, ctb = run_members([b_own, *b_ghosts], basis, a, alive, weights)
    back = exchanged(cts[1:])
    own_ct, *outgoing = pl.pallas_call(
        push_kernel,
        out_shape=[like(8, OWN)] * 5,
        in_specs=vmem(11),
        out_specs=vmem(5),
        compiler_params=params(12),
        name="push",
    )(cts[0], *back, send_lists, basis, geo, live, ctb, a)
    last = exchanged(outgoing)
    new_positions, new_velocities = pl.pallas_call(
        finish_kernel,
        out_shape=[like(3, OWN), like(3, OWN)],
        in_specs=vmem(9) + [pl.BlockSpec(memory_space=pltpu.SMEM)],
        out_specs=vmem(2),
        compiler_params=params(4),
        name="finish",
    )(own_ct, *last, send_lists, positions, velocities, spec, inv_mass)
    return (new_positions, new_velocities)


def solution(mesh):
    split = P(None, ("gx", "gy"))
    row = P(("gx", "gy"))
    placed = (split, split, row, row, split, split) + (P(),) * 10
    return jax.shard_map(
        shards, mesh=mesh, in_specs=placed, out_specs=(split, split), check_vma=False
    )
```

```python
import jax
import jax.numpy as jnp
from jax import lax
from jax.experimental import pallas as pl
from jax.experimental.pallas import tpu as pltpu
from jax.sharding import PartitionSpec as P

SPECIES = 4
RADIAL = 8
FEATS = 40
OWN = 128
SLOTS = 12
EXT = 640
EDGES = SLOTS * OWN
LATENT = 256
MEMBERS = 4
STEP = 256
LAG = 1
MEMBERS_MIB = 32

box_side = 4.0
soft_square = 0.25
centre_step = 0.75
basis_width = 0.75
pool_scale = 0.25
time_step = 0.25

f32 = jnp.float32
bf16 = jnp.bfloat16
NT = (((1,), (1,)), ((), ()))


def vmem(count):
    return [pl.BlockSpec(memory_space=pltpu.VMEM)] * count


def params(mib):
    return pltpu.CompilerParams(vmem_limit_bytes=mib * 1024 * 1024)


def mm(a, b):
    return jnp.dot(a, b, preferred_element_type=f32)


def mm_nt(a, b):
    return lax.dot_general(a, b, NT, preferred_element_type=f32)


def split2(x):
    hi = x.astype(bf16)
    lo = (x - hi.astype(f32)).astype(bf16)
    return hi, lo


def split3(x):
    one = x.astype(bf16).astype(f32)
    rest = x - one
    two = rest.astype(bf16).astype(f32)
    return one, two, rest - two


def stacked3(x, rows):
    parts = list(split3(x))
    left = rows - 3 * x.shape[0]
    if left:
        parts.append(jnp.zeros((left, x.shape[1]), f32))
    return jnp.concatenate(parts, axis=0).astype(bf16)


def unstacked3(x, rows):
    return x[0:rows] + x[rows : 2 * rows] + x[2 * rows : 3 * rows]


def one_hot(rows, index_row, first=0):
    ids = lax.broadcasted_iota(jnp.int32, (rows, index_row.shape[1]), 0) + first
    return (ids == index_row).astype(f32).astype(bf16)


def lists_of(send_ref):
    pairs = ((2, 3), (0, 1), (1, 3), (0, 2))
    return [
        jnp.concatenate([send_ref[a : a + 1, :], send_ref[b : b + 1, :]], axis=1) for a, b in pairs
    ]


def odd_along(axis):
    return lax.rem(lax.axis_index(axis), 2) == 1


def by_partner(plus_x, minus_x, plus_y, minus_y):
    odd_x, odd_y = odd_along("gx"), odd_along("gy")
    return (
        jnp.where(odd_x, plus_x, minus_x),
        jnp.where(odd_x, minus_x, plus_x),
        jnp.where(odd_y, plus_y, minus_y),
        jnp.where(odd_y, minus_y, plus_y),
    )


def by_side(refs):
    s0, s1, s2, s3 = [ref[...] for ref in refs]
    odd_x, odd_y = odd_along("gx"), odd_along("gy")
    return (
        jnp.where(odd_x, s0, s1),
        jnp.where(odd_x, s1, s0),
        jnp.where(odd_y, s2, s3),
        jnp.where(odd_y, s3, s2),
    )


def pack_kernel(pos_hbm, spec_hbm, send_hbm, own_ref, o0, o1, o2, o3, pos_ref, spec_ref, send_ref, sems):
    copies = []
    for n, (given, kept) in enumerate(
        ((pos_hbm, pos_ref), (spec_hbm, spec_ref), (send_hbm, send_ref))
    ):
        copies.append(pltpu.make_async_copy(given, kept, sems.at[n]))
        copies[-1].start()
    for copy in copies:
        copy.wait()
    own = jnp.concatenate(
        [pos_ref[...], spec_ref[...].astype(f32), jnp.zeros((4, OWN), f32)], axis=0
    )
    own_ref[...] = own
    stacked = stacked3(own, 32)
    for out, index in zip((o0, o1, o2, o3), by_partner(*lists_of(send_ref))):
        out[...] = unstacked3(mm(stacked, one_hot(OWN, index)), 8)


def halves(full):
    hi = full.astype(bf16).astype(f32)
    return hi, full - hi


def padded_rows(parts, rows):
    left = rows - sum(part.shape[0] for part in parts)
    return jnp.concatenate(parts + [jnp.zeros((left, parts[0].shape[1]), f32)], axis=0).astype(bf16)


def stack_rows(ref, m, full):
    hi, lo = split2(full)
    ref[m, 0:LATENT] = hi
    ref[m, LATENT : 2 * LATENT] = hi
    ref[m, 2 * LATENT : 3 * LATENT] = lo


def stack_columns(ref, m, full):
    hi, lo = split2(full)
    ref[m, :, 0:LATENT] = hi
    ref[m, :, LATENT : 2 * LATENT] = hi
    ref[m, :, 2 * LATENT :] = lo


def silu_parts(half):
    above = 1.0 + jnp.tanh(half)
    value = half * above
    return value, above + value * (2.0 - above)


def tripled(x):
    hi, lo = split2(x)
    return jnp.concatenate([hi, lo, hi], axis=1)


def picks_kernel(nbr_ref, counts_ref, a_ref, at_ref, live_ref, alive_ref):
    slot_ids = lax.broadcasted_iota(jnp.int32, (SLOTS, OWN), 0)
    live = (slot_ids < counts_ref[...]).astype(f32)
    live_ref[...] = live
    nbr = nbr_ref[...]
    rest = OWN - SLOTS
    columns = jnp.transpose(jnp.concatenate([nbr, jnp.zeros((rest, OWN), jnp.int32)], axis=0))
    alive = jnp.transpose(jnp.concatenate([live, jnp.zeros((rest, OWN), f32)], axis=0))
    lanes = lax.broadcasted_iota(jnp.int32, (OWN, EXT), 1)
    for s in range(SLOTS):
        at = slice(s * OWN, (s + 1) * OWN)
        a_ref[at, :] = (lanes == columns[:, s : s + 1]).astype(f32).astype(bf16)
        at_ref[:, at] = one_hot(EXT, nbr[s : s + 1, :])
        alive_ref[at, :] = jnp.broadcast_to(alive[:, s : s + 1], (OWN, OWN))


def weights_kernel(
    b_ref,
    basis_ref,
    wr1_ref,
    nbr_emb_ref,
    self_emb_ref,
    wr2_ref,
    wout_ref,
    wone_ref,
    wsrc_ref,
    wdst_ref,
    wedge_ref,
    xb_ref,
    bs_ref,
    slope_ref,
    centre_ref,
    weff_ref,
    dst_ref,
    edge_ref,
    dstt_ref,
    eout_ref,
    wback_ref,
    wr2b_ref,
    srct_ref,
):
    hi, lo = halves(b_ref[...])
    tall = jnp.concatenate([hi, lo, hi, jnp.zeros((8, OWN), f32)], axis=0)
    xb = jnp.transpose(tall).astype(bf16)
    xb_ref[...] = xb
    for s in range(SLOTS):
        hi, lo = halves(basis_ref[:, s * OWN : (s + 1) * OWN])
        tall = jnp.concatenate([hi, lo, hi, jnp.zeros((104, OWN), f32)], axis=0)
        bs_ref[s * OWN : (s + 1) * OWN, :] = jnp.transpose(tall).astype(bf16)
    for m in range(MEMBERS):
        mixed = jnp.concatenate(
            [wr1_ref[m] * nbr_emb_ref[m, sp : sp + 1, :] for sp in range(SPECIES)], axis=0
        )
        eff = pool_scale * jnp.dot(
            mixed, wone_ref[m], precision=lax.Precision.HIGHEST, preferred_element_type=f32
        )
        full = 0.5 * jnp.concatenate([eff, self_emb_ref[m], jnp.zeros((4, LATENT), f32)], axis=0)
        hi, lo = halves(full)
        weff = padded_rows([hi, hi, lo], 128)
        weff_ref[m] = weff
        hi, lo = hi[0:32], lo[0:32]
        wback_ref[m, :, 0:LATENT] = padded_rows([hi, lo], 128)
        wback_ref[m, :, LATENT:] = padded_rows([hi], 128)
        hi, lo = halves(wr2_ref[m])
        dst_ref[m, 3 * LATENT :] = padded_rows([0.5 * hi, 0.5 * hi, 0.5 * lo], 128)
        wr2b_ref[:, 2 * m * LATENT : (2 * m + 1) * LATENT] = padded_rows([hi, lo], 128)
        wr2b_ref[:, (2 * m + 1) * LATENT : (2 * m + 2) * LATENT] = padded_rows([hi], 128)
        hid, slope_ref[m] = silu_parts(mm(xb, weff))
        hi, lo = split2(0.5 * wsrc_ref[m])
        centre_ref[m] = mm(tripled(hid), jnp.concatenate([hi, hi, lo], axis=0))
        stack_columns(srct_ref, m, wsrc_ref[m])
        stack_rows(dst_ref, m, 0.5 * wdst_ref[m])
        stack_columns(dstt_ref, m, wdst_ref[m])
        readout = wout_ref[m : m + 1, :] * (0.25 / MEMBERS)
        stack_rows(edge_ref, m, 0.5 * wedge_ref[m])
        stack_columns(eout_ref, m, wedge_ref[m] * readout)


def geometry_kernel(own_ref, g0, g1, g2, g3, send_ref, at_ref, live_ref, b_ref, geo_ref, basis_ref, o0, o1, o2, o3):
    own = own_ref[...]
    rows = lax.broadcasted_iota(jnp.int32, (8, OWN), 0)
    pieces = [own]
    px, mx, py, my = by_side((g0, g1, g2, g3))
    for piece, row, by in ((mx, 0, -box_side), (px, 0, box_side), (my, 1, -box_side), (py, 1, box_side)):
        pieces.append(piece + jnp.where(rows == row, by, 0.0))
    ext = jnp.concatenate(pieces, axis=1)
    there = unstacked3(mm(stacked3(ext, 32), at_ref[...]), 8)
    centres = centre_step * lax.broadcasted_iota(jnp.int32, (RADIAL, OWN), 0).astype(f32)
    sums = [jnp.zeros((RADIAL, OWN), f32) for _ in range(SPECIES)]
    for s in range(SLOTS):
        other = there[:, s * OWN : (s + 1) * OWN]
        sep = other - own
        square = sep[0:1] * sep[0:1] + sep[1:2] * sep[1:2] + sep[2:3] * sep[2:3]
        distance = jnp.sqrt(square + soft_square)
        scaled = (distance - centres) / basis_width
        basis = jnp.exp(-scaled * scaled)
        basis_ref[:, s * OWN : (s + 1) * OWN] = basis
        geo_ref[:, s * OWN : (s + 1) * OWN] = jnp.where(
            rows == 4, distance, jnp.where(rows < 3, sep, other)
        )
        kind = other[3:4]
        alive = live_ref[s : s + 1, :]
        for sp in range(SPECIES):
            sums[sp] = sums[sp] + basis * jnp.where(kind == float(sp), alive, 0.0)
    flags = jnp.where(rows.astype(f32) == own[3:4], 1.0, 0.0)
    b_own = jnp.concatenate(sums + [flags], axis=0)
    b_ref[...] = b_own
    stacked = stacked3(b_own, OWN)
    for out, index in zip((o0, o1, o2, o3), by_partner(*lists_of(send_ref))):
        out[...] = unstacked3(mm(stacked, one_hot(OWN, index)), FEATS)


def main_kernel(
    b1,
    b2,
    b3,
    b4,
    a_ref,
    alive_ref,
    xb_own,
    bs,
    centre_ref,
    weff_ref,
    dst_ref,
    edge_ref,
    dstt_ref,
    eout_ref,
    wback_ref,
    c0,
    c1,
    c2,
    c3,
    c4,
    cx_ref,
    sum_ref,
    xb,
    xe,
    acc,
):
    px, mx, py, my = by_side((b1, b2, b3, b4))
    xb[0:OWN, :] = xb_own[...]
    for n, full in enumerate((mx, px, my, py)):
        hi, lo = halves(full)
        tall = jnp.concatenate([hi, lo, hi, jnp.zeros((8, OWN), f32)], axis=0)
        xb[(n + 1) * OWN : (n + 2) * OWN, :] = jnp.transpose(tall).astype(bf16)
    xe[...] = mm(a_ref[...], xb[...]).astype(bf16)
    acc[...] = jnp.zeros_like(acc)

    def rows_of(t):
        return slice(t * STEP, (t + 1) * STEP)

    def hidden(m, t, v):
        v["z"] = mm(xe[rows_of(t), :], weff_ref[m])

    def hidden_parts(m, t, v):
        hid, v["slope"] = silu_parts(v["z"])
        v["wide"] = tripled(hid)

    def pair(m, t, v):
        v["z"] = mm(v["wide"], dst_ref[m, 0 : 3 * LATENT]) + mm(bs[rows_of(t), :], dst_ref[m, 3 * LATENT :])

    def pair_parts(m, t, v):
        value, v["dx"] = silu_parts(v["z"] + jnp.concatenate([centre_ref[m]] * (STEP // OWN), axis=0))
        v["wide"] = tripled(value)

    def update(m, t, v):
        v["z"] = mm(v["wide"], edge_ref[m])

    def update_parts(m, t, v):
        mask = alive_ref[rows_of(t), :]
        v["wide"] = tripled(silu_parts(v["z"])[1] * jnp.concatenate([mask, mask], axis=1))

    def pull_update(m, t, v):
        v["z"] = mm_nt(v["wide"], eout_ref[m])

    def pull_pair_parts(m, t, v):
        ct = v["z"] * v["dx"]
        v["sum"] = ct[0:OWN]
        for n in range(1, STEP // OWN):
            v["sum"] = v["sum"] + ct[n * OWN : (n + 1) * OWN]
        v["wide"] = tripled(ct)

    def pull_pair(m, t, v):
        cx_ref[rows_of(t), 2 * m * LATENT : (2 * m + 2) * LATENT] = v["wide"][:, 0 : 2 * LATENT]
        v["z"] = mm_nt(v["wide"], dstt_ref[m])

    def pull_hidden_parts(m, t, v):
        hi, lo = split2(v["z"] * v["slope"])
        v["wide"] = jnp.concatenate([hi, lo], axis=1)

    def pull_hidden(m, t, v):
        acc[rows_of(t), :] += mm_nt(v["wide"], wback_ref[m])

    stages = (
        hidden,
        hidden_parts,
        pair,
        pair_parts,
        update,
        update_parts,
        pull_update,
        pull_pair_parts,
        pull_pair,
        pull_hidden_parts,
        pull_hidden,
    )
    tiles = EDGES // STEP
    chains = [(m, t, {}) for m in range(MEMBERS) for t in range(tiles)]
    for tick in range((len(chains) - 1) * LAG + len(stages)):
        for number, chain in enumerate(chains):
            stage = tick - number * LAG
            if 0 <= stage < len(stages):
                stages[stage](*chain)
    for m in range(MEMBERS):
        total = chains[m * tiles][2]["sum"]
        for t in range(1, tiles):
            total = total + chains[m * tiles + t][2]["sum"]
        sum_ref[m] = total

    tall = []
    for s in range(SLOTS):
        wide = jnp.transpose(acc[s * OWN : (s + 1) * OWN, :])
        hi, lo = halves(wide[0:32] + wide[32:64])
        tall.append(jnp.concatenate([hi, lo], axis=0).astype(bf16))
    spread = mm(jnp.concatenate(tall, axis=1), a_ref[...])
    spread = spread[0:32] + spread[32:64]
    blocks = [spread[:, n * OWN : (n + 1) * OWN] for n in range(5)]
    c0[...] = blocks[0]
    for ref, block in zip((c1, c2, c3, c4), by_partner(blocks[2], blocks[1], blocks[4], blocks[3])):
        ref[...] = block


def centre_kernel(c0, cx_ref, sum_ref, slope_ref, srct_ref, wback_ref, wr2b_ref, own_out, ctb_out):
    total = jnp.zeros((OWN, 128), f32)
    for m in range(MEMBERS):
        hi, lo = split2(mm_nt(tripled(sum_ref[m]), srct_ref[m]) * slope_ref[m])
        total = total + mm_nt(jnp.concatenate([hi, lo], axis=1), wback_ref[m])
    wide = jnp.transpose(total)
    own_out[...] = c0[...] + wide[0:32] + wide[32:64]
    ctb = mm_nt(cx_ref[...], wr2b_ref[...])
    for s in range(SLOTS):
        at = slice(s * OWN, (s + 1) * OWN)
        wide = jnp.transpose(ctb[at, :])
        ctb_out[:, at] = wide[0:8] + wide[8:16]


def collected(pieces, send_ref, rows):
    total = None
    for piece, index in zip(pieces, by_partner(*lists_of(send_ref))):
        got = unstacked3(
            mm_nt(stacked3(piece[...], -(-3 * rows // 16) * 16), one_hot(OWN, index)), rows
        )
        total = got if total is None else total + got
    return total


def push_kernel(own_ct, r0, r1, r2, r3, send_ref, basis_ref, geo_ref, live_ref, ctb_ref, a_ref, own_out, o0, o1, o2, o3):
    ct = own_ct[...] + collected((r0, r1, r2, r3), send_ref, 32)
    rows = lax.broadcasted_iota(jnp.int32, (8, OWN), 0)
    centres = centre_step * lax.broadcasted_iota(jnp.int32, (RADIAL, OWN), 0).astype(f32)
    pulled = jnp.zeros((8, OWN), f32)
    seps = []
    for s in range(SLOTS):
        at = slice(s * OWN, (s + 1) * OWN)
        geo = geo_ref[:, at]
        kind = geo[3:4]
        picked = ctb_ref[:, at]
        for sp in range(SPECIES):
            picked = picked + jnp.where(kind == float(sp), ct[sp * 8 : sp * 8 + 8], 0.0)
        distance = geo[4:5]
        slope = picked * basis_ref[:, at] * (distance - centres)
        ct_d = jnp.sum(slope, axis=0, keepdims=True) * (-2.0 / (basis_width * basis_width))
        ct_sep = jnp.where(rows < 3, geo * (ct_d * live_ref[s : s + 1, :] / distance), 0.0)
        pulled = pulled - ct_sep
        seps.append(ct_sep)
    all_sep = jnp.concatenate(seps, axis=1)
    spread = unstacked3(mm(stacked3(all_sep, 32), a_ref[...]), 8)
    own_out[...] = spread[:, 0:OWN] + pulled
    blocks = [spread[:, n * OWN : (n + 1) * OWN] for n in range(5)]
    for out, block in zip((o0, o1, o2, o3), by_partner(blocks[2], blocks[1], blocks[4], blocks[3])):
        out[...] = block


def finish_kernel(own_ct, r0, r1, r2, r3, send_ref, pos_ref, vel_ref, spec_ref, mass_ref, pos_out, vel_out):
    ct = own_ct[...] + collected((r0, r1, r2, r3), send_ref, 8)
    spec = spec_ref[...]
    scale = jnp.zeros(spec.shape, f32)
    for sp in range(SPECIES):
        scale = scale + jnp.where(spec == sp, mass_ref[sp], 0.0)
    vel = vel_ref[...] - time_step * scale * ct[0:3]
    vel_out[...] = vel
    pos_out[...] = pos_ref[...] + time_step * vel


def swapped(shard, axis, first):
    peers = lax.axis_size(axis)
    pairs = []
    for i in range(first, peers + first, 2):
        pairs += [(i % peers, (i + 1) % peers), ((i + 1) % peers, i % peers)]
    return lax.ppermute(shard, axis, pairs)


def exchanged(four):
    return (
        swapped(four[0], "gx", 1),
        swapped(four[1], "gx", 0),
        swapped(four[2], "gy", 1),
        swapped(four[3], "gy", 0),
    )


def like(*shape):
    return jax.ShapeDtypeStruct(shape, f32)


def like16(*shape):
    return jax.ShapeDtypeStruct(shape, bf16)


def run_picks(neighbours, counts):
    return pl.pallas_call(
        picks_kernel,
        out_shape=[
            like16(EDGES, EXT),
            like16(EXT, EDGES),
            like(SLOTS, OWN),
            like(EDGES, OWN),
        ],
        in_specs=vmem(2),
        out_specs=vmem(4),
        compiler_params=params(12),
        cost_estimate=pl.CostEstimate(flops=4_000_000_000, bytes_accessed=16_000_000, transcendentals=0),
        name="picks",
    )(neighbours, counts[None, :])


def run_weights(*given):
    return pl.pallas_call(
        weights_kernel,
        out_shape=[
            like16(OWN, 128),
            like16(EDGES, 128),
            like(MEMBERS, OWN, LATENT),
            like(MEMBERS, OWN, LATENT),
            like16(MEMBERS, 128, LATENT),
            like16(MEMBERS, 3 * LATENT + 128, LATENT),
            like16(MEMBERS, 3 * LATENT, LATENT),
            like16(MEMBERS, LATENT, 3 * LATENT),
            like16(MEMBERS, LATENT, 3 * LATENT),
            like16(MEMBERS, 128, 2 * LATENT),
            like16(128, 2 * MEMBERS * LATENT),
            like16(MEMBERS, LATENT, 3 * LATENT),
        ],
        in_specs=vmem(11),
        out_specs=vmem(12),
        compiler_params=params(12),
        cost_estimate=pl.CostEstimate(flops=4_000_000_000, bytes_accessed=16_000_000, transcendentals=0),
        name="weights",
    )(*given)


def run_members(*given):
    return pl.pallas_call(
        main_kernel,
        out_shape=[like(32, OWN)] * 5
        + [like16(EDGES, 2 * MEMBERS * LATENT), like(MEMBERS, OWN, LATENT)],
        in_specs=vmem(15),
        out_specs=vmem(7),
        scratch_shapes=[
            pltpu.VMEM((EXT, 128), bf16),
            pltpu.VMEM((EDGES, 128), bf16),
            pltpu.VMEM((EDGES, 128), f32),
        ],
        compiler_params=params(MEMBERS_MIB),
        name="members",
    )(*given)


def run_centre(*given):
    return pl.pallas_call(
        centre_kernel,
        out_shape=[like(32, OWN), like(8, EDGES)],
        in_specs=vmem(7),
        out_specs=vmem(2),
        compiler_params=params(16),
        cost_estimate=pl.CostEstimate(flops=3_000_000_000, bytes_accessed=16_000_000, transcendentals=0),
        name="centre",
    )(*given)


def shards(
    positions,
    velocities,
    species,
    counts,
    neighbours,
    send_lists,
    inv_mass,
    w_rad_one,
    emb_nbr,
    emb_self,
    w_one,
    w_src,
    w_dst,
    w_rad_two,
    w_edge,
    w_out,
):
    spec = species[None, :]
    own, *packed = pl.pallas_call(
        pack_kernel,
        out_shape=[like(8, OWN)] * 5,
        in_specs=[pl.BlockSpec(memory_space=pl.ANY)] * 3,
        out_specs=vmem(5),
        scratch_shapes=[
            pltpu.VMEM((3, OWN), f32),
            pltpu.VMEM((1, OWN), jnp.int32),
            pltpu.VMEM((4, OWN // 2), jnp.int32),
            pltpu.SemaphoreType.DMA((3,)),
        ],
        compiler_params=params(60),
        name="pack",
    )(positions, spec, send_lists)
    ghosts = exchanged(packed)
    a, at, live, alive = run_picks(neighbours, counts)
    b_own, geo, basis, *b_packed = pl.pallas_call(
        geometry_kernel,
        out_shape=[like(FEATS, OWN), like(8, EDGES), like(8, EDGES)] + [like(FEATS, OWN)] * 4,
        in_specs=vmem(8),
        out_specs=vmem(7),
        compiler_params=params(12),
        name="geometry",
    )(own, *ghosts, send_lists, at, live)
    b_ghosts = exchanged(b_packed)
    xb, bs, slope, centre, *maps, wback, wr2b, srct = run_weights(
        b_own, basis, w_rad_one, emb_nbr, emb_self, w_rad_two, w_out, w_one, w_src, w_dst, w_edge
    )
    *cts, cx, sums = run_members(*b_ghosts, a, alive, xb, bs, centre, *maps, wback)
    back = exchanged(cts[1:])
    own_sums, ctb = run_centre(cts[0], cx, sums, slope, srct, wback, wr2b)
    own_ct, *outgoing = pl.pallas_call(
        push_kernel,
        out_shape=[like(8, OWN)] * 5,
        in_specs=vmem(11),
        out_specs=vmem(5),
        compiler_params=params(12),
        name="push",
    )(own_sums, *back, send_lists, basis, geo, live, ctb, a)
    last = exchanged(outgoing)
    new_positions, new_velocities = pl.pallas_call(
        finish_kernel,
        out_shape=[like(3, OWN), like(3, OWN)],
        in_specs=vmem(9) + [pl.BlockSpec(memory_space=pltpu.SMEM)],
        out_specs=vmem(2),
        compiler_params=params(4),
        name="finish",
    )(own_ct, *last, send_lists, positions, velocities, spec, inv_mass)
    return (new_positions, new_velocities)


def solution(mesh):
    split = P(None, ("gx", "gy"))
    row = P(("gx", "gy"))
    placed = (split, split, row, row, split, split) + (P(),) * 10
    return jax.shard_map(
        shards, mesh=mesh, in_specs=placed, out_specs=(split, split), check_vma=False
    )
```

```python
import jax
import jax.numpy as jnp
from jax import lax
from jax.experimental import pallas as pl
from jax.experimental.pallas import tpu as pltpu
from jax.sharding import PartitionSpec as P

SPECIES = 4
RADIAL = 8
FEATS = 40
OWN = 128
SLOTS = 12
EXT = 640
EDGES = SLOTS * OWN
LATENT = 256
MEMBERS = 4
STEP = 256
LAG = 1
MEMBERS_MIB = 32

box_side = 4.0
soft_square = 0.25
centre_step = 0.75
basis_width = 0.75
pool_scale = 0.25
time_step = 0.25

f32 = jnp.float32
bf16 = jnp.bfloat16
NT = (((1,), (1,)), ((), ()))


def vmem(count):
    return [pl.BlockSpec(memory_space=pltpu.VMEM)] * count


def params(mib):
    return pltpu.CompilerParams(vmem_limit_bytes=mib * 1024 * 1024)


def mm(a, b):
    return jnp.dot(a, b, preferred_element_type=f32)


def mm_nt(a, b):
    return lax.dot_general(a, b, NT, preferred_element_type=f32)


def split2(x):
    hi = x.astype(bf16)
    lo = (x - hi.astype(f32)).astype(bf16)
    return hi, lo


def split3(x):
    one = x.astype(bf16).astype(f32)
    rest = x - one
    two = rest.astype(bf16).astype(f32)
    return one, two, rest - two


def stacked3(x, rows):
    parts = list(split3(x))
    left = rows - 3 * x.shape[0]
    if left:
        parts.append(jnp.zeros((left, x.shape[1]), f32))
    return jnp.concatenate(parts, axis=0).astype(bf16)


def unstacked3(x, rows):
    return x[0:rows] + x[rows : 2 * rows] + x[2 * rows : 3 * rows]


def one_hot(rows, index_row, first=0):
    ids = lax.broadcasted_iota(jnp.int32, (rows, index_row.shape[1]), 0) + first
    return (ids == index_row).astype(f32).astype(bf16)


def lists_of(send_ref):
    pairs = ((2, 3), (0, 1), (1, 3), (0, 2))
    return [
        jnp.concatenate([send_ref[a : a + 1, :], send_ref[b : b + 1, :]], axis=1) for a, b in pairs
    ]


def odd_along(axis):
    return lax.rem(lax.axis_index(axis), 2) == 1


def by_partner(plus_x, minus_x, plus_y, minus_y):
    odd_x, odd_y = odd_along("gx"), odd_along("gy")
    return (
        jnp.where(odd_x, plus_x, minus_x),
        jnp.where(odd_x, minus_x, plus_x),
        jnp.where(odd_y, plus_y, minus_y),
        jnp.where(odd_y, minus_y, plus_y),
    )


def by_side(refs):
    s0, s1, s2, s3 = [ref[...] for ref in refs]
    odd_x, odd_y = odd_along("gx"), odd_along("gy")
    return (
        jnp.where(odd_x, s0, s1),
        jnp.where(odd_x, s1, s0),
        jnp.where(odd_y, s2, s3),
        jnp.where(odd_y, s3, s2),
    )


def all_lists(send_ref):
    return jnp.concatenate(by_partner(*lists_of(send_ref)), axis=1)


def pack_kernel(pos_hbm, spec_hbm, send_hbm, own_ref, o0, o1, o2, o3, pos_ref, spec_ref, send_ref, sems):
    copies = []
    for n, (given, kept) in enumerate(
        ((pos_hbm, pos_ref), (spec_hbm, spec_ref), (send_hbm, send_ref))
    ):
        copies.append(pltpu.make_async_copy(given, kept, sems.at[n]))
        copies[-1].start()
    for copy in copies:
        copy.wait()
    own = jnp.concatenate(
        [pos_ref[...], spec_ref[...].astype(f32), jnp.zeros((4, OWN), f32)], axis=0
    )
    own_ref[...] = own
    stacked = stacked3(own, 32)
    picked = unstacked3(mm(stacked, one_hot(OWN, all_lists(send_ref))), 8)
    for n, out in enumerate((o0, o1, o2, o3)):
        out[...] = picked[:, n * OWN : (n + 1) * OWN]


def halves(full):
    hi = full.astype(bf16).astype(f32)
    return hi, full - hi


def padded_rows(parts, rows):
    left = rows - sum(part.shape[0] for part in parts)
    return jnp.concatenate(parts + [jnp.zeros((left, parts[0].shape[1]), f32)], axis=0).astype(bf16)


def stack_rows(ref, m, full):
    hi, lo = split2(full)
    ref[m, 0:LATENT] = hi
    ref[m, LATENT : 2 * LATENT] = hi
    ref[m, 2 * LATENT : 3 * LATENT] = lo


def stack_columns(ref, m, full):
    hi, lo = split2(full)
    ref[m, :, 0:LATENT] = hi
    ref[m, :, LATENT : 2 * LATENT] = hi
    ref[m, :, 2 * LATENT :] = lo


def silu_parts(half):
    above = 1.0 + jnp.tanh(half)
    value = half * above
    return value, above + value * (2.0 - above)


def tripled(x):
    hi, lo = split2(x)
    return jnp.concatenate([hi, lo, hi], axis=1)


def picks_kernel(nbr_ref, counts_ref, a_ref, at_ref, live_ref, alive_ref):
    slot_ids = lax.broadcasted_iota(jnp.int32, (SLOTS, OWN), 0)
    live = (slot_ids < counts_ref[...]).astype(f32)
    live_ref[...] = live
    nbr = nbr_ref[...]
    rest = OWN - SLOTS
    columns = jnp.transpose(jnp.concatenate([nbr, jnp.zeros((rest, OWN), jnp.int32)], axis=0))
    alive = jnp.transpose(jnp.concatenate([live, jnp.zeros((rest, OWN), f32)], axis=0))
    lanes = lax.broadcasted_iota(jnp.int32, (OWN, EXT), 1)
    for s in range(SLOTS):
        at = slice(s * OWN, (s + 1) * OWN)
        a_ref[at, :] = (lanes == columns[:, s : s + 1]).astype(f32).astype(bf16)
        at_ref[:, at] = one_hot(EXT, nbr[s : s + 1, :])
        alive_ref[at, :] = jnp.broadcast_to(alive[:, s : s + 1], (OWN, OWN))


def weights_kernel(
    b_ref,
    basis_ref,
    wr1_ref,
    nbr_emb_ref,
    self_emb_ref,
    wr2_ref,
    wout_ref,
    wone_ref,
    wsrc_ref,
    wdst_ref,
    wedge_ref,
    xb_ref,
    bs_ref,
    slope_ref,
    centre_ref,
    weff_ref,
    dst_ref,
    edge_ref,
    dstt_ref,
    eout_ref,
    wback_ref,
    wr2b_ref,
    srct_ref,
):
    hi, lo = halves(b_ref[...])
    tall = jnp.concatenate([hi, lo, hi, jnp.zeros((8, OWN), f32)], axis=0)
    xb = jnp.transpose(tall).astype(bf16)
    xb_ref[...] = xb
    for s in range(SLOTS):
        hi, lo = halves(basis_ref[:, s * OWN : (s + 1) * OWN])
        tall = jnp.concatenate([hi, lo, hi, jnp.zeros((104, OWN), f32)], axis=0)
        bs_ref[s * OWN : (s + 1) * OWN, :] = jnp.transpose(tall).astype(bf16)
    for m in range(MEMBERS):
        mixed = jnp.concatenate(
            [wr1_ref[m] * nbr_emb_ref[m, sp : sp + 1, :] for sp in range(SPECIES)], axis=0
        )
        eff = pool_scale * jnp.dot(
            mixed, wone_ref[m], precision=lax.Precision.HIGHEST, preferred_element_type=f32
        )
        full = 0.5 * jnp.concatenate([eff, self_emb_ref[m], jnp.zeros((4, LATENT), f32)], axis=0)
        hi, lo = halves(full)
        weff = padded_rows([hi, hi, lo], 128)
        weff_ref[m] = weff
        hi, lo = hi[0:32], lo[0:32]
        wback_ref[m, :, 0:LATENT] = padded_rows([hi, lo], 128)
        wback_ref[m, :, LATENT:] = padded_rows([hi], 128)
        hi, lo = halves(wr2_ref[m])
        dst_ref[m, 3 * LATENT :] = padded_rows([0.5 * hi, 0.5 * hi, 0.5 * lo], 128)
        wr2b_ref[:, 2 * m * LATENT : (2 * m + 1) * LATENT] = padded_rows([hi, lo], 128)
        wr2b_ref[:, (2 * m + 1) * LATENT : (2 * m + 2) * LATENT] = padded_rows([hi], 128)
        hid, slope_ref[m] = silu_parts(mm(xb, weff))
        hi, lo = split2(0.5 * wsrc_ref[m])
        centre_ref[m] = mm(tripled(hid), jnp.concatenate([hi, hi, lo], axis=0))
        stack_columns(srct_ref, m, wsrc_ref[m])
        stack_rows(dst_ref, m, 0.5 * wdst_ref[m])
        stack_columns(dstt_ref, m, wdst_ref[m])
        readout = wout_ref[m : m + 1, :] * (0.25 / MEMBERS)
        stack_rows(edge_ref, m, 0.5 * wedge_ref[m])
        stack_columns(eout_ref, m, wedge_ref[m] * readout)


def geometry_kernel(own_ref, g0, g1, g2, g3, send_ref, at_ref, live_ref, b_ref, geo_ref, basis_ref, o0, o1, o2, o3):
    own = own_ref[...]
    rows = lax.broadcasted_iota(jnp.int32, (8, OWN), 0)
    pieces = [own]
    px, mx, py, my = by_side((g0, g1, g2, g3))
    for piece, row, by in ((mx, 0, -box_side), (px, 0, box_side), (my, 1, -box_side), (py, 1, box_side)):
        pieces.append(piece + jnp.where(rows == row, by, 0.0))
    ext = jnp.concatenate(pieces, axis=1)
    there = unstacked3(mm(stacked3(ext, 32), at_ref[...]), 8)
    centres = centre_step * lax.broadcasted_iota(jnp.int32, (RADIAL, OWN), 0).astype(f32)
    sums = [jnp.zeros((RADIAL, OWN), f32) for _ in range(SPECIES)]
    for s in range(SLOTS):
        other = there[:, s * OWN : (s + 1) * OWN]
        sep = other - own
        square = sep[0:1] * sep[0:1] + sep[1:2] * sep[1:2] + sep[2:3] * sep[2:3]
        distance = jnp.sqrt(square + soft_square)
        scaled = (distance - centres) / basis_width
        basis = jnp.exp(-scaled * scaled)
        basis_ref[:, s * OWN : (s + 1) * OWN] = basis
        geo_ref[:, s * OWN : (s + 1) * OWN] = jnp.where(
            rows == 4, distance, jnp.where(rows < 3, sep, other)
        )
        kind = other[3:4]
        alive = live_ref[s : s + 1, :]
        for sp in range(SPECIES):
            sums[sp] = sums[sp] + basis * jnp.where(kind == float(sp), alive, 0.0)
    flags = jnp.where(rows.astype(f32) == own[3:4], 1.0, 0.0)
    b_own = jnp.concatenate(sums + [flags], axis=0)
    b_ref[...] = b_own
    stacked = stacked3(b_own, OWN)
    picked = unstacked3(mm(stacked, one_hot(OWN, all_lists(send_ref))), FEATS)
    for n, out in enumerate((o0, o1, o2, o3)):
        out[...] = picked[:, n * OWN : (n + 1) * OWN]


def main_kernel(
    b1,
    b2,
    b3,
    b4,
    a_ref,
    alive_ref,
    xb_own,
    bs,
    centre_ref,
    weff_ref,
    dst_ref,
    edge_ref,
    dstt_ref,
    eout_ref,
    wback_ref,
    c0,
    c1,
    c2,
    c3,
    c4,
    cx_ref,
    sum_ref,
    xb,
    xe,
    acc,
):
    px, mx, py, my = by_side((b1, b2, b3, b4))
    xb[0:OWN, :] = xb_own[...]
    for n, full in enumerate((mx, px, my, py)):
        hi, lo = halves(full)
        tall = jnp.concatenate([hi, lo, hi, jnp.zeros((8, OWN), f32)], axis=0)
        xb[(n + 1) * OWN : (n + 2) * OWN, :] = jnp.transpose(tall).astype(bf16)
    xe[...] = mm(a_ref[...], xb[...]).astype(bf16)
    acc[...] = jnp.zeros_like(acc)

    def rows_of(t):
        return slice(t * STEP, (t + 1) * STEP)

    def hidden(m, t, v):
        v["z"] = mm(xe[rows_of(t), :], weff_ref[m])

    def hidden_parts(m, t, v):
        hid, v["slope"] = silu_parts(v["z"])
        v["wide"] = tripled(hid)

    def pair(m, t, v):
        v["z"] = mm(v["wide"], dst_ref[m, 0 : 3 * LATENT]) + mm(bs[rows_of(t), :], dst_ref[m, 3 * LATENT :])

    def pair_parts(m, t, v):
        value, v["dx"] = silu_parts(v["z"] + jnp.concatenate([centre_ref[m]] * (STEP // OWN), axis=0))
        v["wide"] = tripled(value)

    def update(m, t, v):
        v["z"] = mm(v["wide"], edge_ref[m])

    def update_parts(m, t, v):
        mask = alive_ref[rows_of(t), :]
        v["wide"] = tripled(silu_parts(v["z"])[1] * jnp.concatenate([mask, mask], axis=1))

    def pull_update(m, t, v):
        v["z"] = mm_nt(v["wide"], eout_ref[m])

    def pull_pair_parts(m, t, v):
        ct = v["z"] * v["dx"]
        v["sum"] = ct[0:OWN]
        for n in range(1, STEP // OWN):
            v["sum"] = v["sum"] + ct[n * OWN : (n + 1) * OWN]
        v["wide"] = tripled(ct)

    def pull_pair(m, t, v):
        cx_ref[rows_of(t), 2 * m * LATENT : (2 * m + 2) * LATENT] = v["wide"][:, 0 : 2 * LATENT]
        v["z"] = mm_nt(v["wide"], dstt_ref[m])

    def pull_hidden_parts(m, t, v):
        hi, lo = split2(v["z"] * v["slope"])
        v["wide"] = jnp.concatenate([hi, lo], axis=1)

    def pull_hidden(m, t, v):
        acc[rows_of(t), :] += mm_nt(v["wide"], wback_ref[m])

    stages = (
        hidden,
        hidden_parts,
        pair,
        pair_parts,
        update,
        update_parts,
        pull_update,
        pull_pair_parts,
        pull_pair,
        pull_hidden_parts,
        pull_hidden,
    )
    tiles = EDGES // STEP
    chains = [(m, t, {}) for m in range(MEMBERS) for t in range(tiles)]
    for tick in range((len(chains) - 1) * LAG + len(stages)):
        for number, chain in enumerate(chains):
            stage = tick - number * LAG
            if 0 <= stage < len(stages):
                stages[stage](*chain)
    for m in range(MEMBERS):
        total = chains[m * tiles][2]["sum"]
        for t in range(1, tiles):
            total = total + chains[m * tiles + t][2]["sum"]
        sum_ref[m] = total

    tall = []
    for s in range(SLOTS):
        wide = jnp.transpose(acc[s * OWN : (s + 1) * OWN, :])
        hi, lo = halves(wide[0:32] + wide[32:64])
        tall.append(jnp.concatenate([hi, lo], axis=0).astype(bf16))
    spread = mm(jnp.concatenate(tall, axis=1), a_ref[...])
    spread = spread[0:32] + spread[32:64]
    blocks = [spread[:, n * OWN : (n + 1) * OWN] for n in range(5)]
    c0[...] = blocks[0]
    for ref, block in zip((c1, c2, c3, c4), by_partner(blocks[2], blocks[1], blocks[4], blocks[3])):
        ref[...] = block


def centre_kernel(
    c0,
    cx_ref,
    sum_ref,
    slope_ref,
    srct_ref,
    wback_ref,
    wr2b_ref,
    spec_ref,
    mass_ref,
    own_out,
    ctb_out,
    step_out,
):
    spec = spec_ref[...]
    scale = jnp.zeros(spec.shape, f32)
    for sp in range(SPECIES):
        scale = scale + jnp.where(spec == sp, mass_ref[sp], 0.0)
    step_out[...] = time_step * scale
    total = jnp.zeros((OWN, 128), f32)
    for m in range(MEMBERS):
        hi, lo = split2(mm_nt(tripled(sum_ref[m]), srct_ref[m]) * slope_ref[m])
        total = total + mm_nt(jnp.concatenate([hi, lo], axis=1), wback_ref[m])
    wide = jnp.transpose(total)
    own_out[...] = c0[...] + wide[0:32] + wide[32:64]
    ctb = mm_nt(cx_ref[...], wr2b_ref[...])
    for s in range(SLOTS):
        at = slice(s * OWN, (s + 1) * OWN)
        wide = jnp.transpose(ctb[at, :])
        ctb_out[:, at] = wide[0:8] + wide[8:16]


def collected(pieces, send_ref, rows):
    wide = jnp.concatenate([piece[...] for piece in pieces], axis=1)
    stacked = stacked3(wide, -(-3 * rows // 16) * 16)
    return unstacked3(mm_nt(stacked, one_hot(OWN, all_lists(send_ref))), rows)


def push_kernel(own_ct, r0, r1, r2, r3, send_ref, basis_ref, geo_ref, live_ref, ctb_ref, a_ref, own_out, o0, o1, o2, o3):
    ct = own_ct[...] + collected((r0, r1, r2, r3), send_ref, 32)
    rows = lax.broadcasted_iota(jnp.int32, (8, OWN), 0)
    centres = centre_step * lax.broadcasted_iota(jnp.int32, (RADIAL, OWN), 0).astype(f32)
    pulled = jnp.zeros((8, OWN), f32)
    seps = []
    for s in range(SLOTS):
        at = slice(s * OWN, (s + 1) * OWN)
        geo = geo_ref[:, at]
        kind = geo[3:4]
        picked = ctb_ref[:, at]
        for sp in range(SPECIES):
            picked = picked + jnp.where(kind == float(sp), ct[sp * 8 : sp * 8 + 8], 0.0)
        distance = geo[4:5]
        slope = picked * basis_ref[:, at] * (distance - centres)
        ct_d = jnp.sum(slope, axis=0, keepdims=True) * (-2.0 / (basis_width * basis_width))
        ct_sep = jnp.where(rows < 3, geo * (ct_d * live_ref[s : s + 1, :] / distance), 0.0)
        pulled = pulled - ct_sep
        seps.append(ct_sep)
    all_sep = jnp.concatenate(seps, axis=1)
    spread = unstacked3(mm(stacked3(all_sep, 32), a_ref[...]), 8)
    own_out[...] = spread[:, 0:OWN] + pulled
    blocks = [spread[:, n * OWN : (n + 1) * OWN] for n in range(5)]
    for out, block in zip((o0, o1, o2, o3), by_partner(blocks[2], blocks[1], blocks[4], blocks[3])):
        out[...] = block


def finish_kernel(own_ct, r0, r1, r2, r3, send_ref, pos_ref, vel_ref, step_ref, pos_out, vel_out):
    ct = own_ct[...] + collected((r0, r1, r2, r3), send_ref, 8)
    vel = vel_ref[...] - step_ref[...] * ct[0:3]
    vel_out[...] = vel
    pos_out[...] = pos_ref[...] + time_step * vel


def swapped(shard, axis, first):
    peers = lax.axis_size(axis)
    pairs = []
    for i in range(first, peers + first, 2):
        pairs += [(i % peers, (i + 1) % peers), ((i + 1) % peers, i % peers)]
    return lax.ppermute(shard, axis, pairs)


def exchanged(four):
    return (
        swapped(four[0], "gx", 1),
        swapped(four[1], "gx", 0),
        swapped(four[2], "gy", 1),
        swapped(four[3], "gy", 0),
    )


def like(*shape):
    return jax.ShapeDtypeStruct(shape, f32)


def like16(*shape):
    return jax.ShapeDtypeStruct(shape, bf16)


def run_picks(neighbours, counts):
    return pl.pallas_call(
        picks_kernel,
        out_shape=[
            like16(EDGES, EXT),
            like16(EXT, EDGES),
            like(SLOTS, OWN),
            like(EDGES, OWN),
        ],
        in_specs=vmem(2),
        out_specs=vmem(4),
        compiler_params=params(12),
        cost_estimate=pl.CostEstimate(flops=4_000_000_000, bytes_accessed=16_000_000, transcendentals=0),
        name="picks",
    )(neighbours, counts[None, :])


def run_weights(*given):
    return pl.pallas_call(
        weights_kernel,
        out_shape=[
            like16(OWN, 128),
            like16(EDGES, 128),
            like(MEMBERS, OWN, LATENT),
            like(MEMBERS, OWN, LATENT),
            like16(MEMBERS, 128, LATENT),
            like16(MEMBERS, 3 * LATENT + 128, LATENT),
            like16(MEMBERS, 3 * LATENT, LATENT),
            like16(MEMBERS, LATENT, 3 * LATENT),
            like16(MEMBERS, LATENT, 3 * LATENT),
            like16(MEMBERS, 128, 2 * LATENT),
            like16(128, 2 * MEMBERS * LATENT),
            like16(MEMBERS, LATENT, 3 * LATENT),
        ],
        in_specs=vmem(11),
        out_specs=vmem(12),
        compiler_params=params(12),
        cost_estimate=pl.CostEstimate(flops=4_000_000_000, bytes_accessed=16_000_000, transcendentals=0),
        name="weights",
    )(*given)


def run_members(*given):
    return pl.pallas_call(
        main_kernel,
        out_shape=[like(32, OWN)] * 5
        + [like16(EDGES, 2 * MEMBERS * LATENT), like(MEMBERS, OWN, LATENT)],
        in_specs=vmem(15),
        out_specs=vmem(7),
        scratch_shapes=[
            pltpu.VMEM((EXT, 128), bf16),
            pltpu.VMEM((EDGES, 128), bf16),
            pltpu.VMEM((EDGES, 128), f32),
        ],
        compiler_params=params(MEMBERS_MIB),
        name="members",
    )(*given)


def run_centre(*given):
    return pl.pallas_call(
        centre_kernel,
        out_shape=[like(32, OWN), like(8, EDGES), like(1, OWN)],
        in_specs=vmem(8) + [pl.BlockSpec(memory_space=pltpu.SMEM)],
        out_specs=vmem(3),
        compiler_params=params(16),
        cost_estimate=pl.CostEstimate(flops=3_000_000_000, bytes_accessed=16_000_000, transcendentals=0),
        name="centre",
    )(*given)


def shards(
    positions,
    velocities,
    species,
    counts,
    neighbours,
    send_lists,
    inv_mass,
    w_rad_one,
    emb_nbr,
    emb_self,
    w_one,
    w_src,
    w_dst,
    w_rad_two,
    w_edge,
    w_out,
):
    spec = species[None, :]
    own, *packed = pl.pallas_call(
        pack_kernel,
        out_shape=[like(8, OWN)] * 5,
        in_specs=[pl.BlockSpec(memory_space=pl.ANY)] * 3,
        out_specs=vmem(5),
        scratch_shapes=[
            pltpu.VMEM((3, OWN), f32),
            pltpu.VMEM((1, OWN), jnp.int32),
            pltpu.VMEM((4, OWN // 2), jnp.int32),
            pltpu.SemaphoreType.DMA((3,)),
        ],
        compiler_params=params(60),
        name="pack",
    )(positions, spec, send_lists)
    ghosts = exchanged(packed)
    a, at, live, alive = run_picks(neighbours, counts)
    b_own, geo, basis, *b_packed = pl.pallas_call(
        geometry_kernel,
        out_shape=[like(FEATS, OWN), like(8, EDGES), like(8, EDGES)] + [like(FEATS, OWN)] * 4,
        in_specs=vmem(8),
        out_specs=vmem(7),
        compiler_params=params(12),
        name="geometry",
    )(own, *ghosts, send_lists, at, live)
    b_ghosts = exchanged(b_packed)
    xb, bs, slope, centre, *maps, wback, wr2b, srct = run_weights(
        b_own, basis, w_rad_one, emb_nbr, emb_self, w_rad_two, w_out, w_one, w_src, w_dst, w_edge
    )
    *cts, cx, sums = run_members(*b_ghosts, a, alive, xb, bs, centre, *maps, wback)
    back = exchanged(cts[1:])
    own_sums, ctb, step = run_centre(
        cts[0], cx, sums, slope, srct, wback, wr2b, spec, inv_mass
    )
    own_ct, *outgoing = pl.pallas_call(
        push_kernel,
        out_shape=[like(8, OWN)] * 5,
        in_specs=vmem(11),
        out_specs=vmem(5),
        compiler_params=params(12),
        name="push",
    )(own_sums, *back, send_lists, basis, geo, live, ctb, a)
    last = exchanged(outgoing)
    new_positions, new_velocities = pl.pallas_call(
        finish_kernel,
        out_shape=[like(3, OWN), like(3, OWN)],
        in_specs=vmem(9),
        out_specs=vmem(2),
        compiler_params=params(4),
        name="finish",
    )(own_ct, *last, send_lists, positions, velocities, step)
    return (new_positions, new_velocities)


def solution(mesh):
    split = P(None, ("gx", "gy"))
    row = P(("gx", "gy"))
    placed = (split, split, row, row, split, split) + (P(),) * 10
    return jax.shard_map(
        shards, mesh=mesh, in_specs=placed, out_specs=(split, split), check_vma=False
    )
```
